512 devices in a mesh: ctx: 64 (over x, z_hi, y, core), ch: 8 (over z_lo).
Axes of the slice: x: 4, y: 4, z: 16 (z_hi: 2, z_lo: 8; z = z_hi * 8 + z_lo), core: 2. Of those that a mesh axis runs over, the one named last changes fastest.
Arguments:
- queries: bfloat16 [256, 8192], P('ch', 'ctx'), may hold values from -6 to 6
- keys: bfloat16 [256, 8192], P('ch', 'ctx'), may hold values from -6 to 6
- values: bfloat16 [256, 8192], P('ch', 'ctx'), may hold values from -6 to 6
- upstream: bfloat16 [256, 8192], P('ch', 'ctx'), may hold values from -6 to 6
- residues: float32 [256, 16], P('ch'), may hold values from -3 to 3
- rates: float32 [256, 16], P('ch'), may hold values from 3.6621093e-06 to 0.05
- w_in: bfloat16 [3, 256, 8192], P(None, 'ch'), may hold values from -0.3125 to 0.3125
Outputs:
- grad_input: bfloat16 [8192, 8192], P('ch', 'ctx')
- grad_residues: float32 [256, 16], P('ch')
- grad_lograte: float32 [256, 16], P('ch')
The draws below stay inside these ranges and needn't reach their ends.
All inputs are finite; a program needn't handle non-finite values.
Results may differ from the reference program's by a relative error of at most 0.017.
Values may be sent and summed in bfloat16 or wider, within the bound.
A program may use at most 64 MiB of HBM per device.

```python
import math
import jax
import jax.numpy as jnp
from jax import lax

D = 8192
CH_DEV = 32
MODES = 16
C = 256
TOKENS = 8192
N_CH = 8


def with_spikes(drawn, stream_key, source, target, parts, factor):
    def block_of(dim):
        return (jnp.arange(drawn.shape[dim]) // (drawn.shape[dim] // parts)).reshape((-1,) + (1,) * (drawn.ndim - 1 - dim))

    near = jax.random.permutation(stream_key, parts)[block_of(target)]
    other_side = (block_of(target) + parts // 2) % parts
    return jnp.where((block_of(source) == near) | (block_of(source) == other_side), factor * drawn, drawn)


def level_of(own_key, shape, shards, least, top_value):
    def one(dim, parts):
        draws = jax.random.uniform(jax.random.fold_in(jax.random.fold_in(own_key, 6), dim), (parts,), jnp.float32, least / len(shards), top_value / len(shards))
        return jnp.repeat(jnp.exp(draws), shape[dim] // parts).reshape((-1,) + (1,) * (len(shape) - dim - 1))

    gain = one(*shards[0])
    for cut in shards[1:]:
        gain = gain * one(*cut)
    return gain


def centred(rng, shape, deviation, bound, split=(), kind=jnp.bfloat16):
    gain = level_of(rng, shape, split, -0.22, 0.18) if split else 1.0
    drawn = jax.random.normal(rng, shape, jnp.float32) * deviation * gain
    return jnp.minimum(jnp.maximum(drawn, -bound), bound).astype(kind)


def bell_draw_with(stream_key, shape, scale, bound, split, heavy, held_as=jnp.bfloat16):
    array = scale * jax.random.normal(stream_key, shape, jnp.float32)
    if split:
        array = array * level_of(stream_key, shape, split, -0.22, 0.18)
    return jnp.clip(with_spikes(array, jax.random.fold_in(stream_key, 3), *heavy), -bound, bound).astype(held_as)


def setup_inputs(seed: int = 0) -> dict:
    splits = jax.random.split(jax.random.key(seed), 8)
    return {
        "queries": centred(splits[0], (C, TOKENS), 1.0, 6.0, ((0, 8), (1, 64))),
        "keys": centred(splits[1], (C, TOKENS), 1.0, 6.0, ((0, 8), (1, 64))),
        "values": centred(splits[2], (C, TOKENS), 1.0, 6.0, ((0, 8), (1, 64))),
        "upstream": centred(splits[3], (C, TOKENS), 1.0, 6.0, ((0, 8), (1, 64))),
        "residues": centred(splits[4], (C, MODES), 0.5, 3.0, ((0, 8),), jnp.float32),
        "rates": jnp.clip(jnp.exp(math.log(0.05) - 9.521739 * jax.random.uniform(splits[5], (C, MODES), jnp.float32) ** level_of(splits[5], (C, MODES), ((0, 8),), -0.2, 0.2)), 3.662109293145477e-06, 0.05),
        "w_in": bell_draw_with(splits[6], (3, C, D), (3 * C) ** -0.5, 0.3125, ((1, 8),), (1, 2, 8, 2.0)),
    }


def reference(queries, keys, values, upstream, residues, rates, w_in):
    total_len = TOKENS
    positions = jnp.arange(total_len, dtype=jnp.int32).astype(jnp.float32)
    mode_gain = jnp.sqrt(2.0 * rates)
    decaying = jnp.exp(-rates[:, :, None] * positions[None, None, :])
    filter_taps = jnp.einsum('cm,cmt->ct', residues * mode_gain, decaying, precision=lax.Precision.HIGHEST)
    key_f = keys.astype(jnp.float32)
    value_f = values.astype(jnp.float32)
    mixed = key_f * value_f
    padded_len = 2 * total_len
    spec_mixed = jnp.fft.rfft(mixed, n=padded_len, axis=1)
    spec_filter = jnp.fft.rfft(filter_taps, n=padded_len, axis=1)
    conv = jnp.fft.irfft(spec_filter * spec_mixed, n=padded_len, axis=1)[:, :total_len]
    dgate = upstream.astype(jnp.float32) * queries.astype(jnp.float32)
    dquery = upstream.astype(jnp.float32) * conv
    spec_grad = jnp.fft.rfft(dgate, n=padded_len, axis=1)
    dmixed = jnp.fft.irfft(jnp.conj(spec_filter) * spec_grad, n=padded_len, axis=1)[:, :total_len]
    dfilter = jnp.fft.irfft(jnp.conj(spec_mixed) * spec_grad, n=padded_len, axis=1)[:, :total_len]
    grad_stack = jnp.stack([dquery, dmixed * value_f, dmixed * key_f]).astype(jnp.bfloat16)
    scale = 1.0 / jnp.sqrt(jnp.float32(total_len))
    grad_residues = jnp.einsum('ct,cmt->cm', dfilter, decaying, precision=lax.Precision.HIGHEST) * mode_gain * scale
    ramp = 0.5 - rates[:, :, None] * positions[None, None, :]
    grad_lograte = residues * mode_gain * jnp.einsum('ct,cmt->cm', dfilter, decaying * ramp, precision=lax.Precision.HIGHEST) * scale
    group_count = N_CH
    grouped_grad = grad_stack.reshape(3, group_count, CH_DEV, total_len).transpose(1, 0, 2, 3)
    grouped_weight = w_in.reshape(3, group_count, CH_DEV, D).transpose(1, 0, 2, 3)

    def add_group(carry, pair):
        grad_part, weight_part = pair
        term = jnp.einsum('act,acd->dt', grad_part.astype(jnp.float32), weight_part.astype(jnp.float32), precision=lax.Precision.HIGHEST)
        return (carry + term.astype(jnp.bfloat16).astype(jnp.float32), None)
    start = jnp.zeros((D, total_len), jnp.float32)
    summed, _ = lax.scan(add_group, start, (grouped_grad, grouped_weight))
    return (summed.astype(jnp.bfloat16), grad_residues, grad_lograte)
```

```python
import functools
import math

import jax
import jax.numpy as jnp
from jax import lax
from jax.experimental import pallas as pl
from jax.experimental.pallas import tpu as pltpu
from jax.sharding import PartitionSpec as P

MESH = pl.DeviceIdType.MESH
HIGHEST = lax.Precision.HIGHEST
F32 = jnp.float32
LANES = 128
HALF = 16


def dot(lhs, rhs, dims=((1,), (0,)), precision=HIGHEST):
    return lax.dot_general(
        lhs, rhs, (dims, ((), ())), precision=precision, preferred_element_type=F32
    )


def dot_nt(lhs, rhs):
    return dot(lhs, rhs, ((1,), (1,)))


def iota(shape, dim):
    return lax.broadcasted_iota(jnp.int32, shape, dim)


def one_where(condition):
    return jnp.where(condition, 1.0, 0.0).astype(F32)


def kernel(
    dims,
    token_count,
    q_ref,
    k_ref,
    v_ref,
    u_ref,
    res_ref,
    rate_ref,
    w_ref,
    out_ref,
    gres_ref,
    glog_ref,
    near_buf,
    far_buf,
    near_sum,
    far_sum,
    dz_buf,
    w_buf,
    own_sem,
    near_send,
    near_recv,
    far_send,
    far_recv,
    nsum_send,
    nsum_recv,
    fsum_send,
    fsum_recv,
    dz_send,
    dz_recv,
    wz_send,
    wz_recv,
    wx_send,
    wx_recv,
    wc_send,
    wc_recv,
):
    nx, nzh, ny, nco, nzl = dims
    nb, na = ny * nco, nx * nzh
    nz = nzh * nzl
    ctx = lax.axis_index("ctx")
    zlo = lax.axis_index("ch")
    near = lax.rem(ctx, nb)
    far = ctx // nb
    core = lax.rem(ctx, nco)
    y = near // nco
    zh = lax.rem(far, nzh)
    x = far // nzh
    z = zh * nzl + zlo
    chans, span = q_ref.shape
    modes = res_ref.shape[1]
    pairs = chans * modes
    blocks = pairs // LANES
    d_len = w_buf.shape[3]

    def ctx_of(px, pzh, py, pco):
        return ((px * nzh + pzh) * ny + py) * nco + pco

    def near_peer(step):
        return {"ctx": far * nb + lax.rem(near + step, nb), "ch": zlo}

    def far_peer(step):
        return {"ctx": lax.rem(far + step, na) * nb + near, "ch": zlo}

    def line_peer(step):
        return {"ctx": ctx, "ch": lax.rem(zlo + step, nzl)}

    def ring_peer(step):
        there = lax.rem(z + step + nz, nz)
        return {"ctx": ctx_of(x, there // nzl, y, core), "ch": lax.rem(there, nzl)}

    def x_peer(step):
        return {"ctx": ctx_of(lax.rem(x + step, nx), zh, y, core), "ch": zlo}

    def y_peer(step):
        return {"ctx": ctx_of(x, zh, lax.rem(y + step, ny), core), "ch": zlo}

    sibling = {"ctx": ctx_of(x, zh, y, lax.rem(core + 1, nco)), "ch": zlo}

    barrier = pltpu.get_barrier_semaphore()
    greeted = 0
    for peer_of, count in ((near_peer, nb), (far_peer, na), (ring_peer, nz)):
        for step in range(1, count):
            pl.semaphore_signal(barrier, inc=1, device_id=peer_of(step), device_id_type=MESH)
            greeted += 1

    own_copy = pltpu.make_async_copy(
        w_ref.at[:, :, pl.ds(pl.multiple_of(zlo * d_len, LANES), d_len)], w_buf.at[0], own_sem
    )
    own_copy.start()

    rates = rate_ref[...]
    gain = jnp.sqrt(2.0 * rates)
    weight = res_ref[...] * gain
    row_chan = one_where(iota((pairs, chans), 0) // modes == iota((pairs, chans), 1))
    row_mode = one_where(lax.rem(iota((pairs, modes), 0), modes) == iota((pairs, modes), 1))
    rate_rows = dot(dot(row_chan, rates) * row_mode, jnp.ones((modes, LANES), F32))
    lane_mode = one_where(iota((modes, pairs), 0) == lax.rem(iota((modes, pairs), 1), modes))
    lane_chan = one_where(iota((chans, pairs), 0) == iota((chans, pairs), 1) // modes)
    spread = dot(jnp.concatenate([rates, weight], axis=0), lane_mode)
    rate_lane = jnp.sum(spread[:chans] * lane_chan, axis=0, keepdims=True)
    weight_diag = spread[chans:] * lane_chan

    def folded(row):
        return [row[:, LANES * i : LANES * (i + 1)] for i in range(blocks)]

    rate4 = jnp.concatenate(folded(rate_lane), axis=0)
    rate8 = jnp.concatenate([rate4, rate4], axis=0)

    time = iota((pairs, span), 1).astype(F32)
    falling = jnp.exp(-rate_rows * time)
    rising = jnp.exp(rate_rows * time)
    chunk_decay = jnp.exp(-float(span) * rate_lane)
    chunk_decay4 = jnp.exp(-float(span) * rate4)

    value_f = v_ref[...].astype(F32)
    key_f = k_ref[...].astype(F32)
    up_f = u_ref[...].astype(F32)
    mixed = key_f * value_f
    dgate = up_f * q_ref[...].astype(F32)

    def diagonal_rows(full):
        return jnp.sum(full * lane_chan, axis=0, keepdims=True)

    steps = iota((chans, span), 1).astype(F32)
    from_mixed = dot_nt(jnp.concatenate([mixed, mixed * (float(span) - steps)], axis=0), rising)
    from_dgate = dot_nt(jnp.concatenate([dgate, dgate * steps], axis=0), falling)
    head = folded(diagonal_rows(from_mixed[:chans]) * chunk_decay) + folded(
        diagonal_rows(from_dgate[:chans])
    )
    state = jnp.concatenate(head, axis=0)
    near_buf[0] = state

    pl.semaphore_wait(barrier, greeted)

    def exchange(buf, send, recv, peer_of, count):
        copies = []
        for step in range(1, count):
            copies.append(
                pltpu.make_async_remote_copy(
                    src_ref=buf.at[0],
                    dst_ref=buf.at[step],
                    send_sem=send.at[step - 1],
                    recv_sem=recv.at[step - 1],
                    device_id=peer_of(step),
                    device_id_type=MESH,
                )
            )
        for copy in copies:
            copy.start()
        return copies

    near_copies = exchange(near_buf, near_send, near_recv, near_peer, nb)

    def half_view(slot, half, column):
        return w_buf.at[
            slot,
            :,
            pl.ds(half * HALF, HALF),
            pl.ds(pl.multiple_of(column * LANES, LANES), LANES),
        ]

    x_column = x * nco + core
    y_column = y * nco + core
    wz_copies = []
    for step in range(1, nzl):
        for half, column in ((0, x_column), (1, y_column)):
            hop = step if step < nzl // 2 + (1 - half) else step - nzl
            peer = ring_peer(hop)
            sem = 2 * (step - 1) + half
            wz_copies.append(
                pltpu.make_async_remote_copy(
                    src_ref=w_ref.at[
                        :,
                        pl.ds(half * HALF, HALF),
                        pl.ds(
                            pl.multiple_of(peer["ch"] * d_len + column * LANES, LANES), LANES
                        ),
                    ],
                    dst_ref=half_view(step, half, column),
                    send_sem=wz_send.at[sem],
                    recv_sem=wz_recv.at[sem],
                    device_id=peer,
                    device_id_type=MESH,
                )
            )
    for copy in wz_copies:
        copy.start()

    def over_modes(values):
        return jnp.broadcast_to(values[:, None, :], (chans, modes, span)).reshape(pairs, span)

    mixed_rows = over_modes(mixed)
    dgate_rows = over_modes(dgate)
    upper = one_where(iota((span, span), 0) <= iota((span, span), 1))
    lower = one_where(iota((span, span), 0) >= iota((span, span), 1))
    forward = falling * dot(rising * mixed_rows, upper)
    backward = rising * dot(falling * dgate_rows, lower)
    conv = dot(weight_diag, forward)
    dmixed = dot(weight_diag, backward)

    is_state = iota((2 * blocks, LANES), 0) < blocks

    def decay(length, if_state, if_other):
        steps_away = jnp.where(is_state, if_state, if_other).astype(F32)
        power = jnp.exp(-float(length) * rate8 * jnp.maximum(steps_away, 0.0))
        return jnp.where(steps_away >= 0.0, power, 0.0)

    before_near, whole_near = [], []
    for step in range(nb):
        other = lax.rem(near - step + nb, nb)
        before_near.append(decay(span, near - 1 - other, other - near - 1))
        whole_near.append(decay(span, nb - 1 - other, other))
    before_far = []
    for step in range(na):
        other = lax.rem(far - step + na, na)
        before_far.append(decay(span * nb, far - 1 - other, other - far - 1))
    inside = decay(span, near, nb - 1 - near)

    for copy in near_copies:
        copy.wait_recv()
    near_total = jnp.zeros_like(state)
    group = jnp.zeros_like(state)
    for step in range(nb):
        arrived = near_buf[step]
        near_total = near_total + before_near[step] * arrived
        group = group + whole_near[step] * arrived
    far_buf[0] = group
    far_copies = exchange(far_buf, far_send, far_recv, far_peer, na)

    for copy in wz_copies:
        copy.wait_recv()

    def column_view(half, column):
        return w_buf.at[
            pl.ds(1, nzl - 1),
            :,
            pl.ds(half * HALF, HALF),
            pl.ds(pl.multiple_of(column * LANES, LANES), LANES),
        ]

    def column_copy(half, column, send, recv, peer):
        view = column_view(half, column)
        return pltpu.make_async_remote_copy(
            src_ref=view,
            dst_ref=view,
            send_sem=send,
            recv_sem=recv,
            device_id=peer,
            device_id_type=MESH,
        )

    wx_copies, wc_copies = [], []
    for half, count, peer_of, column in ((0, nx, x_peer, x_column), (1, ny, y_peer, y_column)):
        for step in range(1, count):
            sem = half * (nx - 1) + step - 1
            wx_copies.append(
                column_copy(half, column, wx_send.at[sem], wx_recv.at[sem], peer_of(step))
            )
            wx_copies[-1].start()
    for half, column in ((0, x_column), (1, y_column)):
        wc_copies.append(column_copy(half, column, wc_send.at[half], wc_recv.at[half], sibling))
        wc_copies[-1].start()

    def lane_sums(rows):
        return dot_nt(jnp.ones((8, span), F32), rows)[0:1]

    same4 = jnp.concatenate(folded(diagonal_rows(dot_nt(dgate, forward))), axis=0)
    apart4 = jnp.concatenate(
        folded(lane_sums((forward - mixed_rows) * backward)), axis=0
    )
    ramp_s4 = jnp.concatenate(
        folded(diagonal_rows(from_mixed[chans:]) * chunk_decay), axis=0
    )
    ramp_g4 = jnp.concatenate(folded(diagonal_rows(from_dgate[chans:])), axis=0)
    s4, g4 = state[:blocks], state[blocks:]

    for copy in far_copies:
        copy.wait_recv()
    far_total = jnp.zeros_like(state)
    for step in range(na):
        far_total = far_total + before_far[step] * far_buf[step]
    entering = near_total + inside * far_total
    before4, after4 = entering[:blocks], entering[blocks:]

    def on_diagonal(rows):
        return weight_diag * jnp.concatenate([rows[i : i + 1] for i in range(blocks)], axis=1)

    conv = conv + dot(on_diagonal(before4), falling)
    dmixed = dmixed + dot(on_diagonal(after4 * chunk_decay4), rising)
    dz_buf[0, 0] = (up_f * conv).astype(jnp.bfloat16)
    dz_buf[0, 1] = (dmixed * value_f).astype(jnp.bfloat16)
    dz_buf[0, 2] = (dmixed * key_f).astype(jnp.bfloat16)
    dz_copies = exchange(dz_buf, dz_send, dz_recv, line_peer, nzl)

    same4 = same4 + g4 * before4
    apart4 = (
        apart4
        + before4 * (ramp_g4 + g4)
        + after4 * (ramp_s4 - s4)
        + float(span) * chunk_decay4 * before4 * after4
    )
    near_sum[0] = jnp.concatenate([same4, apart4], axis=0)
    nsum_copies = exchange(near_sum, nsum_send, nsum_recv, near_peer, nb)

    index = 0
    for half, count, place, base in ((0, nx, x, 0), (1, ny, y, nx - 1)):
        for step in range(1, count):
            wx_copies[index].wait_recv()
            column = lax.rem(place - step + count, count) * nco + core
            sem = 2 + base + step - 1
            wc_copies.append(column_copy(half, column, wc_send.at[sem], wc_recv.at[sem], sibling))
            wc_copies[-1].start()
            index += 1

    for copy in nsum_copies:
        copy.wait_recv()
    total = near_sum[0]
    for step in range(1, nb):
        total = total + near_sum[step]
    far_sum[0] = total
    fsum_copies = exchange(far_sum, fsum_send, fsum_recv, far_peer, na)

    own_copy.wait()
    for copy in wc_copies:
        copy.wait_recv()
    for copy in dz_copies:
        copy.wait_recv()
    rows = nzl * 3 * chans
    product = dot(
        dz_buf[...].reshape(rows, span), w_buf[...].reshape(rows, d_len), ((0,), (0,)), None
    )
    out_ref[...] = product.T.astype(jnp.bfloat16)

    for copy in fsum_copies:
        copy.wait_recv()
    total = far_sum[0]
    for step in range(1, na):
        total = total + far_sum[step]

    def unfolded(rows4):
        row = jnp.concatenate([rows4[i : i + 1] for i in range(blocks)], axis=1)
        return lane_chan * row

    sums = dot_nt(
        jnp.concatenate([unfolded(total[:blocks]), unfolded(total[blocks:])], axis=0), lane_mode
    )
    same, apart = sums[:chans], sums[chans:]
    scale = 1.0 / math.sqrt(float(token_count))
    gres_ref[...] = same * gain * scale
    glog_ref[...] = weight * (0.5 * same - rates * apart) * scale

    for copies in (
        near_copies,
        far_copies,
        wz_copies,
        wx_copies,
        wc_copies,
        dz_copies,
        nsum_copies,
        fsum_copies,
    ):
        for copy in copies:
            copy.wait_send()


def per_device(dims, queries, keys, values, upstream, residues, rates, w_in):
    nx, nzh, ny, nco, nzl = dims
    nb, na = ny * nco, nx * nzh
    chans, span = queries.shape
    modes = residues.shape[1]
    d_len = w_in.shape[2] // nzl
    fold = (2 * chans * modes // LANES, LANES)
    vmem = pl.BlockSpec(memory_space=pltpu.VMEM)
    dma = pltpu.SemaphoreType.DMA
    return pl.pallas_call(
        functools.partial(kernel, dims, span * na * nb),
        out_shape=(
            jax.ShapeDtypeStruct((d_len, span), jnp.bfloat16),
            jax.ShapeDtypeStruct((chans, modes), F32),
            jax.ShapeDtypeStruct((chans, modes), F32),
        ),
        in_specs=[vmem] * 6 + [pl.BlockSpec(memory_space=pl.ANY)],
        out_specs=(vmem, vmem, vmem),
        scratch_shapes=[
            pltpu.VMEM((nb,) + fold, F32),
            pltpu.VMEM((na,) + fold, F32),
            pltpu.VMEM((nb,) + fold, F32),
            pltpu.VMEM((na,) + fold, F32),
            pltpu.VMEM((nzl, 3, chans, span), jnp.bfloat16),
            pltpu.VMEM((nzl, 3, chans, d_len), jnp.bfloat16),
            dma,
            dma((nb - 1,)),
            dma((nb - 1,)),
            dma((na - 1,)),
            dma((na - 1,)),
            dma((nb - 1,)),
            dma((nb - 1,)),
            dma((na - 1,)),
            dma((na - 1,)),
            dma((nzl - 1,)),
            dma((nzl - 1,)),
            dma((2 * (nzl - 1),)),
            dma((2 * (nzl - 1),)),
            dma((nx + ny - 2,)),
            dma((nx + ny - 2,)),
            dma((nx + ny,)),
            dma((nx + ny,)),
        ],
        compiler_params=pltpu.CompilerParams(
            collective_id=0, has_side_effects=True, vmem_limit_bytes=40 * 1024 * 1024
        ),
        cost_estimate=pl.CostEstimate(
            flops=2 * 3 * chans * nzl * d_len * span, bytes_accessed=2 * w_in.size, transcendentals=0
        ),
    )(queries, keys, values, upstream, residues, rates, w_in)


def solution(mesh, dims=(4, 2, 4, 2, 8)):
    return jax.shard_map(
        functools.partial(per_device, dims),
        mesh=mesh,
        in_specs=(
            P("ch", "ctx"),
            P("ch", "ctx"),
            P("ch", "ctx"),
            P("ch", "ctx"),
            P("ch", None),
            P("ch", None),
            P(None, "ch", None),
        ),
        out_specs=(P("ch", "ctx"), P("ch", None), P("ch", None)),
        check_vma=False,
    )
```

```python
import functools
import math

import jax
import jax.numpy as jnp
from jax import lax
from jax.experimental import pallas as pl
from jax.experimental.pallas import tpu as pltpu
from jax.sharding import PartitionSpec as P

MESH = pl.DeviceIdType.MESH
HIGHEST = lax.Precision.HIGHEST
F32 = jnp.float32
LANES = 128
HALF = 16


def dot(lhs, rhs, dims=((1,), (0,)), precision=HIGHEST):
    return lax.dot_general(
        lhs, rhs, (dims, ((), ())), precision=precision, preferred_element_type=F32
    )


def dot_nt(lhs, rhs):
    return dot(lhs, rhs, ((1,), (1,)))


def iota(shape, dim):
    return lax.broadcasted_iota(jnp.int32, shape, dim)


def one_where(condition):
    return jnp.where(condition, 1.0, 0.0).astype(F32)


def chain(first, second, count, length, rate):
    s1, g1, sp1, gp1, a1, b1 = first
    s2, g2, sp2, gp2, a2, b2 = second
    step = jnp.exp(-float(length) * rate)
    whole = jnp.exp(-float(length * count) * rate)
    return (
        step * s1 + s2,
        g1 + whole * g2,
        step * (sp1 + float(length) * s1) + sp2,
        gp1 + whole * (gp2 + float(length * count) * g2),
        a1 + a2 + g2 * s1,
        b1 + b2 + gp2 * s1 + g2 * sp1,
    )


def kernel(
    dims,
    token_count,
    q_hbm,
    k_hbm,
    v_hbm,
    u_hbm,
    res_hbm,
    rate_hbm,
    w_ref,
    out_ref,
    gres_ref,
    glog_ref,
    qkvu_buf,
    small_buf,
    near_buf,
    far_buf,
    dz_buf,
    w_buf,
    in_sem,
    own_sem,
    near_send,
    near_recv,
    far_send,
    far_recv,
    near2_send,
    near2_recv,
    far2_send,
    far2_recv,
    dz_send,
    dz_recv,
    wz_send,
    wz_recv,
    wx_send,
    wx_recv,
    wc_send,
    wc_recv,
):
    nx, nzh, ny, nco, nzl = dims
    nb, na = ny * nco, nx * nzh
    ctx = lax.axis_index("ctx")
    zlo = lax.axis_index("ch")
    near = lax.rem(ctx, nb)
    far = ctx // nb
    core = lax.rem(ctx, nco)
    y = near // nco
    zh = lax.rem(far, nzh)
    x = far // nzh
    chans, span = qkvu_buf.shape[1:]
    modes = small_buf.shape[1]
    pairs = chans * modes
    blocks = pairs // LANES
    d_len = w_buf.shape[3]

    def ctx_of(px, pzh, py, pco):
        return ((px * nzh + pzh) * ny + py) * nco + pco

    def near_peer(away):
        return {"ctx": ctx_of(x, zh, lax.rem(y + away[0], ny), lax.rem(core + away[1], nco)), "ch": zlo}

    def line_peer(step):
        return {"ctx": ctx, "ch": lax.rem(zlo + step, nzl)}

    def x_peer(step):
        return {"ctx": ctx_of(lax.rem(x + step, nx), zh, y, core), "ch": zlo}

    def y_peer(step):
        return {"ctx": ctx_of(x, zh, lax.rem(y + step, ny), core), "ch": zlo}

    def cross_peer(step):
        return {"ctx": ctx_of(lax.rem(x + step, nx), 1 - zh, y, core), "ch": zlo}

    def by_distance(count):
        return sorted(range(count), key=lambda step: -min(step, count - step))

    near_ways = [(dy, dc) for dy in by_distance(ny) for dc in range(nco) if (dy, dc) != (0, 0)]
    x_ways = [step for step in by_distance(nx) if step]
    sibling = {"ctx": ctx_of(x, zh, y, lax.rem(core + 1, nco)), "ch": zlo}

    loads = [
        pltpu.make_async_copy(res_hbm, small_buf.at[0], in_sem.at[4]),
        pltpu.make_async_copy(rate_hbm, small_buf.at[1], in_sem.at[5]),
    ] + [
        pltpu.make_async_copy(ref, qkvu_buf.at[i], in_sem.at[i])
        for i, ref in enumerate((q_hbm, k_hbm, v_hbm, u_hbm))
    ]
    for load in loads:
        load.start()

    barrier = pltpu.get_barrier_semaphore()
    greeted = 0
    for peer_of, steps in ((line_peer, range(1, nzl)), (near_peer, near_ways), (x_peer, x_ways)):
        for step in steps:
            pl.semaphore_signal(barrier, inc=1, device_id=peer_of(step), device_id_type=MESH)
            greeted += 1

    @pl.when(zh == 0)
    def _():
        for step in range(nx):
            pl.semaphore_signal(barrier, inc=1, device_id=cross_peer(step), device_id_type=MESH)

    own_copy = pltpu.make_async_copy(
        w_ref.at[:, :, pl.ds(pl.multiple_of(zlo * d_len, LANES), d_len)], w_buf.at[0], own_sem
    )
    own_copy.start()

    row_chan = one_where(iota((pairs, chans), 0) // modes == iota((pairs, chans), 1))
    row_mode = one_where(lax.rem(iota((pairs, modes), 0), modes) == iota((pairs, modes), 1))
    lane_mode = one_where(iota((modes, pairs), 0) == lax.rem(iota((modes, pairs), 1), modes))
    lane_chan = one_where(iota((chans, pairs), 0) == iota((chans, pairs), 1) // modes)
    time = iota((pairs, span), 1).astype(F32)
    loads[0].wait()
    loads[1].wait()
    rates = small_buf[1]
    gain = jnp.sqrt(2.0 * rates)
    weight = small_buf[0] * gain
    rate_rows = dot(
        dot(row_chan, rates, ((1,), (1,))) * row_mode, jnp.ones((modes, LANES), F32)
    )
    spread = dot(jnp.concatenate([rates, weight], axis=1), lane_mode, ((0,), (0,)))
    rate_lane = jnp.sum(spread[:chans] * lane_chan, axis=0, keepdims=True)
    weight_diag = spread[chans:] * lane_chan

    def folded(row):
        return [row[:, LANES * i : LANES * (i + 1)] for i in range(blocks)]

    def fold(row):
        return jnp.concatenate(folded(row), axis=0)

    def unfold(rows):
        return jnp.concatenate([rows[i : i + 1] for i in range(blocks)], axis=1)

    def diagonal_rows(full):
        return fold(jnp.sum(full * lane_chan, axis=0, keepdims=True))

    rate4 = fold(rate_lane)
    falling = jnp.exp(-rate_rows * time)
    rising = jnp.exp(rate_rows * time)
    chunk_decay = jnp.exp(-float(span) * rate4)

    for load in loads[2:]:
        load.wait()
    key_f = qkvu_buf[1].astype(F32)
    value_f = qkvu_buf[2].astype(F32)
    up_f = qkvu_buf[3].astype(F32)
    mixed = key_f * value_f
    dgate = up_f * qkvu_buf[0].astype(F32)

    s4 = diagonal_rows(dot_nt(mixed, rising)) * chunk_decay
    g4 = diagonal_rows(dot_nt(dgate, falling))
    near_buf[near, 0 : 2 * blocks] = jnp.concatenate([s4, g4], axis=0)

    pl.semaphore_wait(barrier, jnp.where(zh == 0, greeted, greeted + nx))

    def make(src, dst, send, recv, peer):
        return pltpu.make_async_remote_copy(
            src_ref=src,
            dst_ref=dst,
            send_sem=send,
            recv_sem=recv,
            device_id=peer,
            device_id_type=MESH,
        )

    first, rest = pl.ds(0, 2 * blocks), pl.ds(2 * blocks, 4 * blocks)

    def near_exchange(part, send, recv):
        view = near_buf.at[near, part]
        return [
            make(view, view, send.at[i], recv.at[i], near_peer(way))
            for i, way in enumerate(near_ways)
        ]

    def far_exchange(part, send, recv):
        view = far_buf.at[far, part]
        same = [
            make(view, view, send.at[step - 1], recv.at[step - 1], x_peer(step))
            for step in x_ways
        ]
        cross = [
            make(view, view, send.at[nx - 1 + step], recv.at[nx - 1 + step], cross_peer(step))
            for step in by_distance(nx)
        ]
        return same, cross

    def start(copies):
        for copy in copies:
            copy.start()

    def arrive(copies):
        for copy in copies:
            copy.wait_recv()

    near_copies = near_exchange(first, near_send, near_recv)
    start(near_copies)

    def half_view(slot, half, column):
        return w_buf.at[
            slot,
            :,
            pl.ds(half * HALF, HALF),
            pl.ds(pl.multiple_of(column * LANES, LANES), LANES),
        ]

    x_column = x * nco + core
    y_column = y * nco + core
    wz_copies = []
    for step in range(1, nzl):
        for half, column in ((0, x_column), (1, y_column)):
            peer = line_peer(step)
            sem = 2 * (step - 1) + half
            source = w_ref.at[
                :,
                pl.ds(half * HALF, HALF),
                pl.ds(pl.multiple_of(peer["ch"] * d_len + column * LANES, LANES), LANES),
            ]
            wz_copies.append(
                make(source, half_view(step, half, column), wz_send.at[sem], wz_recv.at[sem], peer)
            )
    start(wz_copies)

    def over_modes(values):
        return jnp.broadcast_to(values[:, None, :], (chans, modes, span)).reshape(pairs, span)

    def lane_sums(rows):
        return fold(dot_nt(jnp.ones((8, span), F32), rows)[0:1])

    mixed_rows = over_modes(mixed)
    dgate_rows = over_modes(dgate)
    upper = one_where(iota((span, span), 0) <= iota((span, span), 1))
    lower = one_where(iota((span, span), 0) >= iota((span, span), 1))
    forward = falling * dot(rising * mixed_rows, upper)
    backward = rising * dot(falling * dgate_rows, lower)
    conv = dot(weight_diag, forward)
    dmixed = dot(weight_diag, backward)

    steps = iota((chans, span), 1).astype(F32)
    near_buf[near, 2 * blocks : 6 * blocks] = jnp.concatenate(
        [
            diagonal_rows(dot_nt(mixed * (float(span) - steps), rising)) * chunk_decay,
            diagonal_rows(dot_nt(dgate * steps, falling)),
            diagonal_rows(dot_nt(dgate, forward)),
            lane_sums((forward - mixed_rows) * backward),
        ],
        axis=0,
    )
    near2_copies = near_exchange(rest, near2_send, near2_recv)
    start(near2_copies)

    def scan(pieces, here, decay):
        run = jnp.zeros_like(decay)
        before = run
        for i, (s, _) in enumerate(pieces):
            before = jnp.where(here == i, run, before)
            run = decay * run + s
        back = jnp.zeros_like(decay)
        after = back
        for i, (_, g) in reversed(list(enumerate(pieces))):
            after = jnp.where(here == i, back, after)
            back = decay * back + g
        return before, after, run, back

    def states_of(buf, count):
        return [(buf[i, 0:blocks], buf[i, blocks : 2 * blocks]) for i in range(count)]

    arrive(near_copies)
    near_states = states_of(near_buf, nb)
    before_near, after_near, s_group, g_group = scan(near_states, near, chunk_decay)
    far_buf[far, 0 : 2 * blocks] = jnp.concatenate([s_group, g_group], axis=0)
    same_copies, cross_copies = far_exchange(first, far_send, far_recv)

    @pl.when(zh == 1)
    def _():
        start(cross_copies)

    start(same_copies)

    def pieces_of(buf, count):
        return [
            tuple(buf[i, j * blocks : (j + 1) * blocks] for j in range(6)) for i in range(count)
        ]

    def chained(pieces, length):
        total = pieces[0]
        for i in range(1, len(pieces)):
            total = chain(total, pieces[i], i, length, rate4)
        return total

    arrive(near2_copies)
    group = chained(pieces_of(near_buf, nb), span)
    far_buf[far, 2 * blocks : 6 * blocks] = jnp.concatenate(group[2:], axis=0)
    same2_copies, cross2_copies = far_exchange(rest, far2_send, far2_recv)

    @pl.when(zh == 1)
    def _():
        start(cross2_copies)

    start(same2_copies)

    arrive(wz_copies)

    def column_copy(half, column, send, recv, peer):
        view = w_buf.at[
            pl.ds(1, nzl - 1),
            :,
            pl.ds(half * HALF, HALF),
            pl.ds(pl.multiple_of(column * LANES, LANES), LANES),
        ]
        return make(view, view, send, recv, peer)

    wx_copies, wc_copies = [], []
    for half, count, peer_of, column in ((0, nx, x_peer, x_column), (1, ny, y_peer, y_column)):
        for step in range(1, count):
            sem = half * (nx - 1) + step - 1
            wx_copies.append(
                column_copy(half, column, wx_send.at[sem], wx_recv.at[sem], peer_of(step))
            )
    start(wx_copies)
    for half, column in ((0, x_column), (1, y_column)):
        wc_copies.append(column_copy(half, column, wc_send.at[half], wc_recv.at[half], sibling))
    start(wc_copies)

    arrive(same_copies)
    arrive(cross_copies)

    @pl.when(zh == 0)
    def _():
        start(cross_copies)
        start(cross2_copies)

    before_far, after_far, _, _ = scan(
        states_of(far_buf, na), far, jnp.exp(-float(span * nb) * rate4)
    )
    from_start = (near * span).astype(F32)
    to_end = ((nb - 1 - near) * span).astype(F32)
    before = before_near + jnp.exp(-rate4 * from_start) * before_far
    after = after_near + jnp.exp(-rate4 * to_end) * after_far

    conv = conv + dot(weight_diag * unfold(before), falling)
    dmixed = dmixed + dot(weight_diag * unfold(after * chunk_decay), rising)
    dz_buf[0, 0] = (up_f * conv).astype(jnp.bfloat16)
    dz_buf[0, 1] = (dmixed * value_f).astype(jnp.bfloat16)
    dz_buf[0, 2] = (dmixed * key_f).astype(jnp.bfloat16)
    dz_copies = [
        make(dz_buf.at[0], dz_buf.at[step], dz_send.at[step - 1], dz_recv.at[step - 1], line_peer(step))
        for step in range(1, nzl)
    ]
    start(dz_copies)

    index = 0
    for half, count, place, base in ((0, nx, x, 0), (1, ny, y, nx - 1)):
        for step in range(1, count):
            wx_copies[index].wait_recv()
            column = lax.rem(place - step + count, count) * nco + core
            sem = 2 + base + step - 1
            wc_copies.append(column_copy(half, column, wc_send.at[sem], wc_recv.at[sem], sibling))
            wc_copies[-1].start()
            index += 1

    arrive(same2_copies)
    arrive(cross2_copies)
    total = chained(pieces_of(far_buf, na), span * nb)
    sums = dot_nt(
        lane_mode,
        jnp.concatenate([lane_chan * unfold(total[4]), lane_chan * unfold(total[5])], axis=0),
    )
    same, apart = sums[:, :chans], sums[:, chans:]
    scale = 1.0 / math.sqrt(float(token_count))
    gres_ref[...] = same * gain * scale
    glog_ref[...] = weight * (0.5 * same - rates * apart) * scale

    own_copy.wait()
    arrive(wc_copies)
    arrive(dz_copies)
    rows = nzl * 3 * chans
    product = dot(
        dz_buf[...].reshape(rows, span), w_buf[...].reshape(rows, d_len), ((0,), (0,)), None
    )
    out_ref[...] = product.T.astype(jnp.bfloat16)

    for copies in (
        near_copies,
        near2_copies,
        same_copies,
        cross_copies,
        same2_copies,
        cross2_copies,
        wz_copies,
        wx_copies,
        wc_copies,
        dz_copies,
    ):
        for copy in copies:
            copy.wait_send()


def per_device(dims, queries, keys, values, upstream, residues, rates, w_in):
    nx, nzh, ny, nco, nzl = dims
    nb, na = ny * nco, nx * nzh
    chans, span = queries.shape
    modes = residues.shape[1]
    d_len = w_in.shape[2] // nzl
    states = (6 * chans * modes // LANES, LANES)
    vmem = pl.BlockSpec(memory_space=pltpu.VMEM)
    dma = pltpu.SemaphoreType.DMA
    outs = (
        jax.ShapeDtypeStruct((d_len, span), jnp.bfloat16),
        jax.ShapeDtypeStruct((modes, chans), F32),
        jax.ShapeDtypeStruct((modes, chans), F32),
    )
    grad_input, grad_residues, grad_lograte = pl.pallas_call(
        functools.partial(kernel, dims, span * na * nb),
        out_shape=outs,
        in_specs=[pl.BlockSpec(memory_space=pltpu.HBM)] * 7,
        out_specs=(vmem, vmem, vmem),
        scratch_shapes=[
            pltpu.VMEM((4, chans, span), jnp.bfloat16),
            pltpu.VMEM((2, modes, chans), F32),
            pltpu.VMEM((nb,) + states, F32),
            pltpu.VMEM((na,) + states, F32),
            pltpu.VMEM((nzl, 3, chans, span), jnp.bfloat16),
            pltpu.VMEM((nzl, 3, chans, d_len), jnp.bfloat16),
            dma((6,)),
            dma,
            dma((nb - 1,)),
            dma((nb - 1,)),
            dma((na - 1,)),
            dma((na - 1,)),
            dma((nb - 1,)),
            dma((nb - 1,)),
            dma((na - 1,)),
            dma((na - 1,)),
            dma((nzl - 1,)),
            dma((nzl - 1,)),
            dma((2 * (nzl - 1),)),
            dma((2 * (nzl - 1),)),
            dma((nx + ny - 2,)),
            dma((nx + ny - 2,)),
            dma((nx + ny,)),
            dma((nx + ny,)),
        ],
        compiler_params=pltpu.CompilerParams(
            collective_id=0, has_side_effects=True, vmem_limit_bytes=40 * 1024 * 1024
        ),
        cost_estimate=pl.CostEstimate(
            flops=2 * 3 * chans * nzl * d_len * span, bytes_accessed=2 * w_in.size, transcendentals=0
        ),
    )(*[pltpu.with_memory_space_constraint(a, pltpu.HBM) for a in (queries, keys, values, upstream, residues.T, rates.T, w_in)])
    return grad_input, grad_residues.T, grad_lograte.T


def solution(mesh, dims=(4, 2, 4, 2, 8)):
    return jax.shard_map(
        functools.partial(per_device, dims),
        mesh=mesh,
        in_specs=(
            P("ch", "ctx"),
            P("ch", "ctx"),
            P("ch", "ctx"),
            P("ch", "ctx"),
            P("ch", None),
            P("ch", None),
            P(None, "ch", None),
        ),
        out_specs=(P("ch", "ctx"), P("ch", None), P("ch", None)),
        check_vma=False,
    )
```

```python
import functools
import math

import jax
import jax.numpy as jnp
from jax import lax
from jax.experimental import pallas as pl
from jax.experimental.pallas import tpu as pltpu
from jax.sharding import PartitionSpec as P

MESH = pl.DeviceIdType.MESH
HIGHEST = lax.Precision.HIGHEST
F32 = jnp.float32
LANES = 128
HALF = 16
CLOSE = 3


def dot(lhs, rhs, dims=((1,), (0,)), precision=HIGHEST):
    return lax.dot_general(
        lhs, rhs, (dims, ((), ())), precision=precision, preferred_element_type=F32
    )


def dot_nt(lhs, rhs):
    return dot(lhs, rhs, ((1,), (1,)))


def split(values):
    high = values.astype(jnp.bfloat16)
    return high, (values - high.astype(F32)).astype(jnp.bfloat16)


def dot_split(lhs, rhs, dims=((1,), (0,))):
    high, low = split(lhs)
    rows = lhs.shape[0]
    both = dot(jnp.concatenate([high, low], axis=0), rhs[0], dims, None)
    return both[:rows] + both[rows:] + dot(high, rhs[1], dims, None)


def iota(shape, dim):
    return lax.broadcasted_iota(jnp.int32, shape, dim)


def one_where(condition):
    return jnp.where(condition, 1.0, 0.0).astype(F32)


def chain(first, second, count, length, rate):
    s1, g1, sp1, gp1, a1, b1 = first
    s2, g2, sp2, gp2, a2, b2 = second
    step = jnp.exp(-float(length) * rate)
    whole = jnp.exp(-float(length * count) * rate)
    return (
        step * s1 + s2,
        g1 + whole * g2,
        step * (sp1 + float(length) * s1) + sp2,
        gp1 + whole * (gp2 + float(length * count) * g2),
        a1 + a2 + g2 * s1,
        b1 + b2 + gp2 * s1 + g2 * sp1,
    )


def kernel(dims, token_count, semaphores, *refs):
    nx, nzh, ny, nco, nzl = dims
    nb, na = ny * nco, nx * nzh
    q_hbm, k_hbm, v_hbm, u_hbm, res_hbm, rate_hbm, w_ref, out_ref, gres_ref, glog_ref = refs[:10]
    small_buf, raw_buf, half_buf, far_buf, state_buf, late_buf, dz_buf, w_buf = refs[10:18]
    sems = dict(zip(semaphores, refs[18:]))
    ctx = lax.axis_index("ctx")
    zlo = lax.axis_index("ch")
    near = lax.rem(ctx, nb)
    far = ctx // nb
    core = lax.rem(ctx, nco)
    y = near // nco
    zh = lax.rem(far, nzh)
    x = far // nzh
    chans, span = raw_buf.shape[2:]
    modes = small_buf.shape[1]
    pairs = chans * modes
    blocks = pairs // LANES
    d_len = w_buf.shape[3]

    def ctx_of(px, pzh, py, pco):
        return ((px * nzh + pzh) * ny + py) * nco + pco

    def plane_peer(away):
        dx, dy, dc = away
        there = ctx_of(lax.rem(x + dx, nx), zh, lax.rem(y + dy, ny), lax.rem(core + dc, nco))
        return {"ctx": there, "ch": zlo}

    def line_peer(step):
        return {"ctx": ctx, "ch": lax.rem(zlo + step, nzl)}

    def x_peer(step):
        return {"ctx": ctx_of(lax.rem(x + step, nx), zh, y, core), "ch": zlo}

    def y_peer(step):
        return {"ctx": ctx_of(x, zh, lax.rem(y + step, ny), core), "ch": zlo}

    def by_distance(count):
        return sorted(range(count), key=lambda step: -min(step, count - step))

    def hops(away):
        return min(away[0], nx - away[0]) + min(away[1], ny - away[1])

    plane_ways = sorted(
        [(i, j, k) for i in range(nx) for j in range(ny) for k in range(nco)][1:],
        key=lambda away: -hops(away),
    )
    x_ways = [step for step in by_distance(nx) if step]
    y_ways = [step for step in by_distance(ny) if step]
    line_ways = list(range(1, nzl))
    sibling = plane_peer((0, 0, 1))
    twin = {"ctx": ctx_of(x, 1 - zh, y, core), "ch": zlo}

    loads = [
        pltpu.make_async_copy(res_hbm, small_buf.at[0], sems["load"].at[4]),
        pltpu.make_async_copy(rate_hbm, small_buf.at[1], sems["load"].at[5]),
    ] + [
        pltpu.make_async_copy(ref, raw_buf.at[0, i], sems["load"].at[i])
        for i, ref in enumerate((q_hbm, k_hbm, v_hbm, u_hbm))
    ]
    for load in loads:
        load.start()

    barrier = pltpu.get_barrier_semaphore()

    def greet(semaphore, peer):
        pl.semaphore_signal(semaphore, inc=1, device_id=peer, device_id_type=MESH)

    def on_line(offset):
        return jnp.logical_and(zlo + offset >= 0, zlo + offset < nzl)

    def line_at(offset):
        return {"ctx": ctx, "ch": zlo + offset}

    def greet_line(semaphore, offsets, also=True):
        for offset in offsets:
            pl.when(jnp.logical_and(on_line(offset), also))(
                functools.partial(greet, semaphore, line_at(offset))
            )

    def count_line(offsets):
        return sum(on_line(offset).astype(jnp.int32) for offset in offsets)

    close = [sign * d for d in range(1, CLOSE + 1) for sign in (1, -1)]
    apart_ways = [sign * d for d in range(CLOSE + 1, nzl) for sign in (1, -1)]
    greet_line(barrier, close)
    greet_line(barrier, apart_ways, zh == 0)
    for way in plane_ways:
        greet(barrier, plane_peer(way))

    @pl.when(zh == 0)
    def _():
        greet(barrier, twin)

    greeted = len(plane_ways) + jnp.where(zh == 0, nzl - 1, 1 + count_line(close))

    def make(src, dst, name, index, peer):
        return pltpu.make_async_remote_copy(
            src_ref=src,
            dst_ref=dst,
            send_sem=sems[name + "_send"].at[index],
            recv_sem=sems[name + "_recv"].at[index],
            device_id=peer,
            device_id_type=MESH,
        )

    def same_place(view, name, peer_of, ways, base=0):
        return [make(view, view, name, base + i, peer_of(way)) for i, way in enumerate(ways)]

    def start(copies):
        for copy in copies:
            copy.start()

    def arrive(copies):
        for copy in copies:
            copy.wait_recv()

    def folded(row):
        return [row[:, LANES * i : LANES * (i + 1)] for i in range(blocks)]

    def fold(row):
        return jnp.concatenate(folded(row), axis=0)

    def unfold(rows):
        return jnp.concatenate([rows[i : i + 1] for i in range(blocks)], axis=1)

    lane_mode = one_where(iota((modes, pairs), 0) == lax.rem(iota((modes, pairs), 1), modes))
    lane_chan = one_where(iota((chans, pairs), 0) == iota((chans, pairs), 1) // modes)
    time = iota((pairs, span), 1).astype(F32)
    upper = one_where(iota((span, span), 0) <= iota((span, span), 1)).astype(jnp.bfloat16)
    lower = one_where(iota((span, span), 0) >= iota((span, span), 1)).astype(jnp.bfloat16)

    def lane_sum(full):
        return jnp.sum(full * lane_chan, axis=0, keepdims=True)

    def diagonal_rows(full):
        return fold(lane_sum(full))

    def over_modes(values):
        return jnp.broadcast_to(values[:, None, :], (chans, modes, span)).reshape(pairs, span)

    def powers(rate_lane):
        high = rate_lane.astype(jnp.bfloat16).astype(F32)
        middle = (rate_lane - high).astype(jnp.bfloat16).astype(F32)
        parts = [high, middle, rate_lane - high - middle, jnp.zeros((HALF - 3, pairs), F32)]
        column = jnp.concatenate(parts, axis=0).astype(jnp.bfloat16)
        ones = jnp.ones((HALF, span), jnp.bfloat16)
        exponent = dot(column, ones, ((0,), (0,)), None) * time
        return jnp.exp(-exponent), jnp.exp(exponent)

    def sums_along(values, ones):
        high, low = split(values)
        return dot(high, ones, precision=None) + dot(low, ones, precision=None)

    nt = ((1,), (1,))

    loads[0].wait()
    loads[1].wait()
    rates = small_buf[1]
    gain = jnp.sqrt(2.0 * rates)
    weight = small_buf[0] * gain
    spread = dot(jnp.concatenate([rates, weight], axis=1), lane_mode, ((0,), (0,)))
    rate_lane = lane_sum(spread[:chans])
    weight_lane = lane_sum(spread[chans:])
    rate4, weight4 = fold(rate_lane), fold(weight_lane)
    falling, rising = powers(rate_lane)
    chunk_decay = jnp.exp(-float(span) * rate4)

    for load in loads[2:]:
        load.wait()
    query_f, key_f, value_f, up_f = (raw_buf[0, i].astype(F32) for i in range(4))
    mixed = key_f * value_f
    dgate = up_f * query_f
    falling_parts, rising_parts = split(falling), split(rising)
    s4 = diagonal_rows(dot_split(mixed, rising_parts, nt)) * chunk_decay
    g4 = diagonal_rows(dot_split(dgate, falling_parts, nt))
    here = x * nb + near
    half_buf[here, 0 : 2 * blocks] = jnp.concatenate([s4, g4], axis=0)

    pl.semaphore_wait(barrier, greeted)

    first, rest = pl.ds(0, 2 * blocks), pl.ds(2 * blocks, 4 * blocks)
    plane_copies = same_place(half_buf.at[here, first], "plane", plane_peer, plane_ways)
    start(plane_copies)

    @pl.when(zh == 1)
    def _():
        greet_line(sems["first"], (CLOSE, -CLOSE))

    per_core = nzl // nco
    half = x // (nx // 2)
    column = lax.rem(x, nx // 2) * ny + y

    def part_rows(rows_half):
        return pl.ds(pl.multiple_of(rows_half * HALF, HALF), HALF)

    def columns(begin, count):
        return pl.ds(pl.multiple_of(begin * LANES, LANES), count * LANES)

    def source_part(owner):
        return w_ref.at[:, part_rows(half), columns(owner * (d_len // LANES) + column, 1)]

    def part_of(slot):
        return w_buf.at[slot, :, part_rows(half), columns(column, 1)]

    own_part = pltpu.make_async_copy(source_part(zlo), part_of(0), sems["own"].at[0])
    wz_copies = []
    for i in range(per_core):
        slot = core * per_core + i
        peer = line_peer(slot)
        wz_copies.append(make(source_part(peer["ch"]), part_of(slot), "wz", i, peer))
    part = pl.ds(1, 2)
    kv_copies = [
        make(raw_buf.at[0, part], raw_buf.at[k, part], "kv", k - 1, line_peer(k)) for k in line_ways
    ]

    @pl.when(core == 0)
    def _():
        own_part.start()

    def start_line():
        pl.when(core != 0)(wz_copies[0].start)
        start(wz_copies[1:])
        start(kv_copies)

    pl.when(zh == 0)(start_line)

    mixed_rows = over_modes(mixed)
    forward = falling * sums_along(rising * mixed_rows, upper)
    backward = rising * sums_along(falling * over_modes(dgate), lower)
    forward_parts = split(forward)
    weight_diag = lane_chan * weight_lane
    conv = dot_split(weight_diag, forward_parts)
    dmixed = dot_split(weight_diag, split(backward))
    steps = iota((chans, span), 1).astype(F32)
    apart = split((forward - mixed_rows) * backward)
    ones = jnp.ones((HALF, span), jnp.bfloat16)
    apart_lane = (dot(ones, apart[0], nt, None) + dot(ones, apart[1], nt, None))[0:1]
    half_buf[here, 2 * blocks : 6 * blocks] = jnp.concatenate(
        [
            diagonal_rows(dot_split(mixed * (float(span) - steps), rising_parts, nt)) * chunk_decay,
            diagonal_rows(dot_split(dgate * steps, falling_parts, nt)),
            diagonal_rows(dot_split(dgate, forward_parts, nt)),
            fold(apart_lane),
        ],
        axis=0,
    )
    plane2_copies = same_place(half_buf.at[here, rest], "plane2", plane_peer, plane_ways)
    start(plane2_copies)

    @pl.when(zh == 1)
    def _():
        pl.semaphore_wait(sems["first"], count_line((CLOSE, -CLOSE)))
        greet_line(sems["second"], (CLOSE + 1, -CLOSE - 1))

    rate8 = jnp.concatenate([rate4, rate4], axis=0)
    is_state = iota((2 * blocks, LANES), 0) < blocks

    def decay(length, if_state, if_other):
        away = jnp.where(is_state, if_state, if_other).astype(F32)
        power = jnp.exp(-float(length) * rate8 * jnp.maximum(away, 0.0))
        return jnp.where(away >= 0.0, power, 0.0)

    group_len = span * nb
    to_own, to_opp = [], []
    for px in range(nx):
        ahead = nzh * (x - px)
        to_own.append(decay(group_len, ahead - 1, -ahead - 1))
        to_opp.append(decay(group_len, ahead - 2 * zh, -ahead + 2 * zh - 2))
    inside = decay(span, near, nb - 1 - near)
    use = jnp.concatenate([weight4, weight4 * chunk_decay], axis=0)

    def group_states(px):
        run = jnp.zeros_like(rate4)
        back = run
        before = run
        after = run
        for i in range(nb):
            before = jnp.where(near == i, run, before)
            run = chunk_decay * run + half_buf[px * nb + i, 0:blocks]
            j = nb - 1 - i
            after = jnp.where(near == j, back, after)
            back = chunk_decay * back + half_buf[px * nb + j, blocks : 2 * blocks]
        return jnp.concatenate([before, after], axis=0), jnp.concatenate([run, back], axis=0)

    arrive(plane_copies)
    own_states = jnp.zeros_like(rate8)
    opp_states = jnp.zeros_like(rate8)
    from_near = jnp.zeros_like(rate8)
    for px in range(nx):
        around, states = group_states(px)
        from_near = jnp.where(x == px, around, from_near)
        own_states = own_states + to_own[px] * states
        opp_states = opp_states + to_opp[px] * states
    state_buf[zh] = inside * opp_states
    twin_copies = [make(state_buf.at[zh], state_buf.at[zh], "twin", 0, twin)]

    @pl.when(zh == 1)
    def _():
        start(twin_copies)
        pl.semaphore_wait(sems["second"], count_line((CLOSE + 1, -CLOSE - 1)))
        start_line()

    def chained(pieces, length):
        total = pieces[0]
        for i in range(1, len(pieces)):
            total = chain(total, pieces[i], i, length, rate4)
        return total

    def piece(rows):
        return tuple(rows[j * blocks : (j + 1) * blocks] for j in range(6))

    arrive(plane2_copies)
    for px in range(nx):
        group = chained([piece(half_buf[px * nb + i]) for i in range(nb)], span)
        far_buf[zh, px] = jnp.concatenate(group, axis=0)
    twin2_copies = [make(far_buf.at[zh], far_buf.at[zh], "twin", 1, twin)]

    @pl.when(zh == 1)
    def _():
        start(twin2_copies)

    two = per_core // 2
    begin = core * per_core

    def across(slots, rows, cols):
        return w_buf.at[pl.ds(slots, two), :, rows, cols]

    x_peers = [(way, 0, 0) for way in x_ways]
    y_peers = [(0, way, 0) for way in y_ways]
    my_part = (part_rows(half), columns(column, 1))
    w2_copies = same_place(across(begin, *my_part), "w2", plane_peer, x_peers)
    w2_copies += same_place(across(begin + two, *my_part), "w2", plane_peer, y_peers, nx - 1)
    w3_copies = []
    for i in range(nx // 2):
        view = across(begin, pl.ds(0, 2 * HALF), columns(i * ny + y, 1))
        w3_copies += same_place(view, "w3", plane_peer, y_peers, i * (ny - 1))
    view = across(begin + two, part_rows(half), columns(lax.rem(x, nx // 2) * ny, ny))
    w3_copies += same_place(view, "w3", plane_peer, x_peers, nx // 2 * (ny - 1))
    whole = w_buf.at[pl.ds(begin, per_core)]
    w4_copies = [make(whole, whole, "w4", 0, sibling)]

    @pl.when(core == 0)
    def _():
        own_part.wait()

    @pl.when(core != 0)
    def _():
        wz_copies[0].wait_recv()

    arrive(wz_copies[1:])
    start(w2_copies)

    arrive(twin_copies)

    @pl.when(zh == 0)
    def _():
        start(twin_copies)
        start(twin2_copies)

    states = use * (from_near + inside * own_states + state_buf[1 - zh])
    conv = conv + dot_split(lane_chan * unfold(states[:blocks]), falling_parts)
    dmixed = dmixed + dot_split(lane_chan * unfold(states[blocks:]), rising_parts)
    late_buf[0, 0] = (up_f * conv).astype(jnp.bfloat16)
    late_buf[0, 1] = dmixed.astype(jnp.bfloat16)
    late_copies = [make(late_buf.at[0], late_buf.at[k], "late", k - 1, line_peer(k)) for k in line_ways]
    start(late_copies)
    dz_buf[0, 0] = late_buf[0, 0]
    dz_buf[0, 1] = (dmixed * value_f).astype(jnp.bfloat16)
    dz_buf[0, 2] = (dmixed * key_f).astype(jnp.bfloat16)

    arrive(w2_copies)
    start(w3_copies)
    arrive(w3_copies)
    start(w4_copies)

    arrive(kv_copies)
    arrive(w4_copies)
    arrive(late_copies)
    for k in line_ways:
        dmixed_k = late_buf[k, 1].astype(F32)
        dz_buf[k, 0] = late_buf[k, 0]
        dz_buf[k, 1] = (dmixed_k * raw_buf[k, 2].astype(F32)).astype(jnp.bfloat16)
        dz_buf[k, 2] = (dmixed_k * raw_buf[k, 1].astype(F32)).astype(jnp.bfloat16)
    rows = nzl * 3 * chans
    product = dot(
        dz_buf[...].reshape(rows, span), w_buf[...].reshape(rows, d_len), ((0,), (0,)), None
    )
    out_ref[...] = product.T.astype(jnp.bfloat16)

    arrive(twin2_copies)
    pieces = [piece(far_buf[h, px]) for px in range(nx) for h in range(nzh)]
    total = chained(pieces, group_len)
    sums = dot_nt(
        lane_mode,
        jnp.concatenate([lane_chan * unfold(total[4]), lane_chan * unfold(total[5])], axis=0),
    )
    same, apart = sums[:, :chans], sums[:, chans:]
    scale = 1.0 / math.sqrt(float(token_count))
    gres_ref[...] = same * gain * scale
    glog_ref[...] = weight * (0.5 * same - rates * apart) * scale

    @pl.when(core != 0)
    def _():
        wz_copies[0].wait_send()

    for copies in (
        plane_copies,
        plane2_copies,
        twin_copies,
        twin2_copies,
        wz_copies[1:],
        kv_copies,
        late_copies,
        w2_copies,
        w3_copies,
        w4_copies,
    ):
        for copy in copies:
            copy.wait_send()


def per_device(dims, queries, keys, values, upstream, residues, rates, w_in):
    nx, nzh, ny, nco, nzl = dims
    nb, na = ny * nco, nx * nzh
    chans, span = queries.shape
    modes = residues.shape[1]
    d_len = w_in.shape[2] // nzl
    pairs = chans * modes
    blocks = pairs // LANES
    vmem = pl.BlockSpec(memory_space=pltpu.VMEM)
    counts = {
        "plane": nx * nb - 1,
        "plane2": nx * nb - 1,
        "twin": 2,
        "wz": nzl // nco,
        "kv": nzl - 1,
        "late": nzl - 1,
        "w2": nx + ny - 2,
        "w3": nx // 2 * (ny - 1) + nx - 1,
        "w4": 1,
    }
    semaphores = {"load": 6, "own": 1}
    for name, count in counts.items():
        semaphores[name + "_send"] = count
        semaphores[name + "_recv"] = count
    arrays = [
        pltpu.with_memory_space_constraint(array, pltpu.HBM)
        for array in (queries, keys, values, upstream, residues.T, rates.T, w_in)
    ]
    grad_input, grad_residues, grad_lograte = pl.pallas_call(
        functools.partial(kernel, dims, span * na * nb, (*semaphores, "first", "second")),
        out_shape=(
            jax.ShapeDtypeStruct((d_len, span), jnp.bfloat16),
            jax.ShapeDtypeStruct((modes, chans), F32),
            jax.ShapeDtypeStruct((modes, chans), F32),
        ),
        in_specs=[pl.BlockSpec(memory_space=pltpu.HBM)] * 7,
        out_specs=(vmem, vmem, vmem),
        scratch_shapes=[
            pltpu.VMEM((2, modes, chans), F32),
            pltpu.VMEM((nzl, 4, chans, span), jnp.bfloat16),
            pltpu.VMEM((nx * nb, 6 * blocks, LANES), F32),
            pltpu.VMEM((nzh, nx, 6 * blocks, LANES), F32),
            pltpu.VMEM((nzh, 2 * blocks, LANES), F32),
            pltpu.VMEM((nzl, 2, chans, span), jnp.bfloat16),
            pltpu.VMEM((nzl, 3, chans, span), jnp.bfloat16),
            pltpu.VMEM((nzl, 3, chans, d_len), jnp.bfloat16),
        ]
        + [pltpu.SemaphoreType.DMA((count,)) for count in semaphores.values()]
        + [pltpu.SemaphoreType.REGULAR] * 2,
        compiler_params=pltpu.CompilerParams(
            collective_id=0, has_side_effects=True, vmem_limit_bytes=40 * 1024 * 1024
        ),
        cost_estimate=pl.CostEstimate(
            flops=2 * 3 * chans * nzl * d_len * span, bytes_accessed=2 * w_in.size, transcendentals=0
        ),
    )(*arrays)
    return grad_input, grad_residues.T, grad_lograte.T


def solution(mesh, dims=(4, 2, 4, 2, 8)):
    return jax.shard_map(
        functools.partial(per_device, dims),
        mesh=mesh,
        in_specs=(
            P("ch", "ctx"),
            P("ch", "ctx"),
            P("ch", "ctx"),
            P("ch", "ctx"),
            P("ch", None),
            P("ch", None),
            P(None, "ch", None),
        ),
        out_specs=(P("ch", "ctx"), P("ch", None), P("ch", None)),
        check_vma=False,
    )
```

```python
import functools
import math

import jax
import jax.numpy as jnp
from jax import lax
from jax.experimental import pallas as pl
from jax.experimental.pallas import tpu as pltpu
from jax.sharding import PartitionSpec as P

MESH = pl.DeviceIdType.MESH
HIGHEST = lax.Precision.HIGHEST
F32 = jnp.float32
LANES = 128
HALF = 16
CLOSE = 3


def dot(lhs, rhs, dims=((1,), (0,)), precision=HIGHEST):
    return lax.dot_general(
        lhs, rhs, (dims, ((), ())), precision=precision, preferred_element_type=F32
    )


def dot_nt(lhs, rhs):
    return dot(lhs, rhs, ((1,), (1,)))


def split(values):
    high = values.astype(jnp.bfloat16)
    return high, (values - high.astype(F32)).astype(jnp.bfloat16)


def dot_split(lhs, rhs, dims=((1,), (0,))):
    high, low = split(lhs)
    rows = lhs.shape[0]
    both = dot(jnp.concatenate([high, low], axis=0), rhs[0], dims, None)
    return both[:rows] + both[rows:] + dot(high, rhs[1], dims, None)


def iota(shape, dim):
    return lax.broadcasted_iota(jnp.int32, shape, dim)


def one_where(condition):
    return jnp.where(condition, 1.0, 0.0).astype(F32)


def chain(first, second, count, length, rate):
    s1, g1, sp1, gp1, a1, b1 = first
    s2, g2, sp2, gp2, a2, b2 = second
    step = jnp.exp(-float(length) * rate)
    whole = jnp.exp(-float(length * count) * rate)
    return (
        step * s1 + s2,
        g1 + whole * g2,
        step * (sp1 + float(length) * s1) + sp2,
        gp1 + whole * (gp2 + float(length * count) * g2),
        a1 + a2 + g2 * s1,
        b1 + b2 + gp2 * s1 + g2 * sp1,
    )


def kernel(dims, token_count, semaphores, *refs):
    nx, nzh, ny, nco, nzl = dims
    nb, na = ny * nco, nx * nzh
    q_hbm, k_hbm, v_hbm, u_hbm, res_hbm, rate_hbm, w_ref, out_ref, gres_ref, glog_ref = refs[:10]
    small_buf, raw_buf, half_buf, state_buf, tuple_buf, total_buf, late_buf, dz_buf, w_buf = refs[10:19]
    sems = dict(zip(semaphores, refs[19:]))
    ctx = lax.axis_index("ctx")
    zlo = lax.axis_index("ch")
    near = lax.rem(ctx, nb)
    far = ctx // nb
    core = lax.rem(ctx, nco)
    y = near // nco
    zh = lax.rem(far, nzh)
    x = far // nzh
    chans, span = raw_buf.shape[2:]
    modes = small_buf.shape[1]
    pairs = chans * modes
    blocks = pairs // LANES
    d_len = w_buf.shape[3]

    def ctx_of(px, pzh, py, pco):
        return ((px * nzh + pzh) * ny + py) * nco + pco

    def plane_peer(away):
        dx, dy, dc = away
        there = ctx_of(lax.rem(x + dx, nx), zh, lax.rem(y + dy, ny), lax.rem(core + dc, nco))
        return {"ctx": there, "ch": zlo}

    def line_peer(step):
        return {"ctx": ctx, "ch": lax.rem(zlo + step, nzl)}

    def x_peer(step):
        return {"ctx": ctx_of(lax.rem(x + step, nx), zh, y, core), "ch": zlo}

    def y_peer(step):
        return {"ctx": ctx_of(x, zh, lax.rem(y + step, ny), core), "ch": zlo}

    def by_distance(count):
        return sorted(range(count), key=lambda step: -min(step, count - step))

    def hops(away):
        return min(away[0], nx - away[0]) + min(away[1], ny - away[1])

    plane_ways = sorted(
        [(i, j, k) for i in range(nx) for j in range(ny) for k in range(nco)][1:],
        key=lambda away: -hops(away),
    )
    x_ways = [step for step in by_distance(nx) if step]
    y_ways = [step for step in by_distance(ny) if step]
    line_ways = list(range(1, nzl))
    sibling = plane_peer((0, 0, 1))
    near_ways = [way for way in plane_ways if way[0] == 0]
    twin = {"ctx": ctx_of(x, 1 - zh, y, core), "ch": zlo}

    def member(group):
        return {"ctx": group * nb + near, "ch": zlo}

    collects = near == far
    far_target = lax.rem(near, nzh)

    loads = [
        pltpu.make_async_copy(res_hbm, small_buf.at[0], sems["load"].at[4]),
        pltpu.make_async_copy(rate_hbm, small_buf.at[1], sems["load"].at[5]),
    ] + [
        pltpu.make_async_copy(ref, raw_buf.at[0, i], sems["load"].at[i])
        for i, ref in enumerate((q_hbm, k_hbm, v_hbm, u_hbm))
    ]
    for load in loads:
        load.start()

    barrier = pltpu.get_barrier_semaphore()

    def greet(semaphore, peer):
        pl.semaphore_signal(semaphore, inc=1, device_id=peer, device_id_type=MESH)

    def on_line(offset):
        return jnp.logical_and(zlo + offset >= 0, zlo + offset < nzl)

    def line_at(offset):
        return {"ctx": ctx, "ch": zlo + offset}

    def greet_line(semaphore, offsets, also=True):
        for offset in offsets:
            pl.when(jnp.logical_and(on_line(offset), also))(
                functools.partial(greet, semaphore, line_at(offset))
            )

    def count_line(offsets):
        return sum(on_line(offset).astype(jnp.int32) for offset in offsets)

    close = [sign * d for d in range(1, CLOSE + 1) for sign in (1, -1)]
    apart_ways = [sign * d for d in range(CLOSE + 1, nzl) for sign in (1, -1)]
    greet_line(barrier, close)
    greet_line(barrier, apart_ways, zh == 0)
    for way in plane_ways:
        greet(barrier, plane_peer(way))

    @pl.when(zh == 0)
    def _():
        greet(barrier, twin)

        @pl.when(collects)
        def _():
            for px in range(nx):
                greet(barrier, member(px * nzh + 1))

        pl.when(far_target == 1)(functools.partial(greet, barrier, member(near)))

    from_first = 1 + jnp.where(far_target == 0, 1, 0) + jnp.where(collects, nx, 0)
    greeted = len(plane_ways) + jnp.where(zh == 0, nzl - 1, from_first + count_line(close))

    def make(src, dst, name, index, peer):
        return pltpu.make_async_remote_copy(
            src_ref=src,
            dst_ref=dst,
            send_sem=sems[name + "_send"].at[index],
            recv_sem=sems[name + "_recv"].at[index],
            device_id=peer,
            device_id_type=MESH,
        )

    def same_place(view, name, peer_of, ways, base=0):
        return [make(view, view, name, base + i, peer_of(way)) for i, way in enumerate(ways)]

    def start(copies):
        for copy in copies:
            copy.start()

    def arrive(copies):
        for copy in copies:
            copy.wait_recv()

    def folded(row):
        return [row[:, LANES * i : LANES * (i + 1)] for i in range(blocks)]

    def fold(row):
        return jnp.concatenate(folded(row), axis=0)

    def unfold(rows):
        return jnp.concatenate([rows[i : i + 1] for i in range(blocks)], axis=1)

    lane_mode = one_where(iota((modes, pairs), 0) == lax.rem(iota((modes, pairs), 1), modes))
    lane_chan = one_where(iota((chans, pairs), 0) == iota((chans, pairs), 1) // modes)
    time = iota((pairs, span), 1).astype(F32)
    upper = one_where(iota((span, span), 0) <= iota((span, span), 1)).astype(jnp.bfloat16)
    lower = one_where(iota((span, span), 0) >= iota((span, span), 1)).astype(jnp.bfloat16)

    def lane_sum(full):
        return jnp.sum(full * lane_chan, axis=0, keepdims=True)

    def diagonal_rows(full):
        return fold(lane_sum(full))

    def over_modes(values):
        return jnp.broadcast_to(values[:, None, :], (chans, modes, span)).reshape(pairs, span)

    def powers(rate_lane):
        high = rate_lane.astype(jnp.bfloat16).astype(F32)
        middle = (rate_lane - high).astype(jnp.bfloat16).astype(F32)
        parts = [high, middle, rate_lane - high - middle, jnp.zeros((HALF - 3, pairs), F32)]
        column = jnp.concatenate(parts, axis=0).astype(jnp.bfloat16)
        ones = jnp.ones((HALF, span), jnp.bfloat16)
        exponent = dot(column, ones, ((0,), (0,)), None) * time
        return jnp.exp(-exponent), jnp.exp(exponent)

    def sums_along(values, ones):
        high, low = split(values)
        return dot(high, ones, precision=None) + dot(low, ones, precision=None)

    nt = ((1,), (1,))

    loads[0].wait()
    loads[1].wait()
    rates = small_buf[1]
    gain = jnp.sqrt(2.0 * rates)
    weight = small_buf[0] * gain
    spread = dot(jnp.concatenate([rates, weight], axis=1), lane_mode, ((0,), (0,)))
    rate_lane = lane_sum(spread[:chans])
    weight_lane = lane_sum(spread[chans:])
    rate4, weight4 = fold(rate_lane), fold(weight_lane)
    falling, rising = powers(rate_lane)
    chunk_decay = jnp.exp(-float(span) * rate4)

    for load in loads[2:]:
        load.wait()
    query_f, key_f, value_f, up_f = (raw_buf[0, i].astype(F32) for i in range(4))
    mixed = key_f * value_f
    dgate = up_f * query_f
    falling_parts, rising_parts = split(falling), split(rising)
    s4 = diagonal_rows(dot_split(mixed, rising_parts, nt)) * chunk_decay
    g4 = diagonal_rows(dot_split(dgate, falling_parts, nt))
    here = x * nb + near
    first, rest = pl.ds(0, 2 * blocks), pl.ds(2 * blocks, 4 * blocks)
    half_buf[here, 0 : 2 * blocks] = jnp.concatenate([s4, g4], axis=0)

    pl.semaphore_wait(barrier, greeted)

    plane_copies = same_place(half_buf.at[here, first], "plane", plane_peer, plane_ways)

    start(plane_copies)

    @pl.when(zh == 1)
    def _():
        greet_line(sems["first"], (CLOSE, -CLOSE))

        @pl.when(collects)
        def _():
            for px in range(nx):
                greet(sems["third"], member(px * nzh))

    per_core = nzl // nco
    half = x // (nx // 2)
    column = lax.rem(x, nx // 2) * ny + y

    def part_rows(rows_half):
        return pl.ds(pl.multiple_of(rows_half * HALF, HALF), HALF)

    def columns(begin, count):
        return pl.ds(pl.multiple_of(begin * LANES, LANES), count * LANES)

    def source_part(owner):
        return w_ref.at[:, part_rows(half), columns(owner * (d_len // LANES) + column, 1)]

    def part_of(slot):
        return w_buf.at[slot, :, part_rows(half), columns(column, 1)]

    own_part = pltpu.make_async_copy(source_part(zlo), part_of(0), sems["own"].at[0])
    wz_copies = []
    for i in range(per_core):
        slot = core * per_core + i
        peer = line_peer(slot)
        wz_copies.append(make(source_part(peer["ch"]), part_of(slot), "wz", i, peer))
    part = pl.ds(1, 2)
    kv_copies = [
        make(raw_buf.at[0, part], raw_buf.at[k, part], "kv", k - 1, line_peer(k)) for k in line_ways
    ]

    @pl.when(core == 0)
    def _():
        own_part.start()

    def start_line():
        pl.when(core != 0)(wz_copies[0].start)
        start(wz_copies[1:])
        start(kv_copies)

    pl.when(zh == 0)(start_line)

    mixed_rows = over_modes(mixed)
    forward = falling * sums_along(rising * mixed_rows, upper)
    backward = rising * sums_along(falling * over_modes(dgate), lower)
    forward_parts = split(forward)
    weight_diag = lane_chan * weight_lane
    conv = dot_split(weight_diag, forward_parts)
    dmixed = dot_split(weight_diag, split(backward))
    steps = iota((chans, span), 1).astype(F32)
    apart = split((forward - mixed_rows) * backward)
    ones = jnp.ones((HALF, span), jnp.bfloat16)
    apart_lane = (dot(ones, apart[0], nt, None) + dot(ones, apart[1], nt, None))[0:1]
    half_buf[here, 2 * blocks : 6 * blocks] = jnp.concatenate(
        [
            diagonal_rows(dot_split(mixed * (float(span) - steps), rising_parts, nt)) * chunk_decay,
            diagonal_rows(dot_split(dgate * steps, falling_parts, nt)),
            diagonal_rows(dot_split(dgate, forward_parts, nt)),
            fold(apart_lane),
        ],
        axis=0,
    )
    near_copies = same_place(half_buf.at[here, rest], "near", plane_peer, near_ways)
    start(near_copies)

    @pl.when(zh == 1)
    def _():
        pl.semaphore_wait(sems["first"], count_line((CLOSE, -CLOSE)))
        greet_line(sems["second"], (CLOSE + 1, -CLOSE - 1))

    rate8 = jnp.concatenate([rate4, rate4], axis=0)
    is_state = iota((2 * blocks, LANES), 0) < blocks

    def decay(length, if_state, if_other):
        away = jnp.where(is_state, if_state, if_other).astype(F32)
        power = jnp.exp(-float(length) * rate8 * jnp.maximum(away, 0.0))
        return jnp.where(away >= 0.0, power, 0.0)

    group_len = span * nb
    to_own, to_opp = [], []
    for px in range(nx):
        ahead = nzh * (x - px)
        to_own.append(decay(group_len, ahead - 1, -ahead - 1))
        to_opp.append(decay(group_len, ahead - 2 * zh, -ahead + 2 * zh - 2))
    inside = decay(span, near, nb - 1 - near)
    use = jnp.concatenate([weight4, weight4 * chunk_decay], axis=0)

    def group_states(px):
        run = jnp.zeros_like(rate4)
        back = run
        before = run
        after = run
        for i in range(nb):
            before = jnp.where(near == i, run, before)
            run = chunk_decay * run + half_buf[px * nb + i, 0:blocks]
            j = nb - 1 - i
            after = jnp.where(near == j, back, after)
            back = chunk_decay * back + half_buf[px * nb + j, blocks : 2 * blocks]
        return jnp.concatenate([before, after], axis=0), jnp.concatenate([run, back], axis=0)

    arrive(plane_copies)
    far_states = jnp.zeros_like(rate8)
    twin_states = jnp.zeros_like(rate8)
    from_near = jnp.zeros_like(rate8)
    for px in range(nx):
        around, states = group_states(px)
        from_near = jnp.where(x == px, around, from_near)
        far_states = far_states + to_own[px] * states
        twin_states = twin_states + to_opp[px] * states
    state_buf[zh] = twin_states
    twin_copies = [make(state_buf.at[zh], state_buf.at[zh], "twin", 0, twin)]

    @pl.when(zh == 1)
    def _():
        start(twin_copies)
        pl.semaphore_wait(sems["second"], count_line((CLOSE + 1, -CLOSE - 1)))
        start_line()

    def chained(pieces, length):
        total = pieces[0]
        for i in range(1, len(pieces)):
            total = chain(total, pieces[i], i, length, rate4)
        return total

    def piece(rows):
        return tuple(rows[j * blocks : (j + 1) * blocks] for j in range(6))

    arrive(near_copies)
    pieces = [piece(half_buf[x * nb + i]) for i in range(nb)]
    tuple_buf[far] = jnp.concatenate(chained(pieces, span), axis=0)
    tuple_copy = make(tuple_buf.at[far], tuple_buf.at[far], "tuple", far, member(near))
    hands_on = jnp.logical_not(collects)
    waits = jnp.logical_and(zh == 0, far_target == 1)
    pl.when(jnp.logical_and(hands_on, jnp.logical_not(waits)))(tuple_copy.start)

    two = per_core // 2
    begin = core * per_core

    def across(slots, rows, cols):
        return w_buf.at[pl.ds(slots, two), :, rows, cols]

    x_peers = [(way, 0, 0) for way in x_ways]
    y_peers = [(0, way, 0) for way in y_ways]
    my_part = (part_rows(half), columns(column, 1))
    w2_copies = same_place(across(begin, *my_part), "w2", plane_peer, x_peers)
    w2_copies += same_place(across(begin + two, *my_part), "w2", plane_peer, y_peers, nx - 1)
    w3_copies = []
    for i in range(nx // 2):
        view = across(begin, pl.ds(0, 2 * HALF), columns(i * ny + y, 1))
        w3_copies += same_place(view, "w3", plane_peer, y_peers, i * (ny - 1))
    view = across(begin + two, part_rows(half), columns(lax.rem(x, nx // 2) * ny, ny))
    w3_copies += same_place(view, "w3", plane_peer, x_peers, nx // 2 * (ny - 1))
    whole = w_buf.at[pl.ds(begin, per_core)]
    w4_copies = [make(whole, whole, "w4", 0, sibling)]

    pl.when(core == 0)(own_part.wait)
    pl.when(core != 0)(wz_copies[0].wait_recv)
    arrive(wz_copies[1:])
    start(w2_copies)
    arrive(w2_copies)
    start(w3_copies)
    arrive(twin_copies)

    @pl.when(zh == 0)
    def _():
        start(twin_copies)

    states = use * (from_near + inside * (far_states + state_buf[1 - zh]))
    conv = conv + dot_split(lane_chan * unfold(states[:blocks]), falling_parts)
    dmixed = dmixed + dot_split(lane_chan * unfold(states[blocks:]), rising_parts)
    late_buf[0, 0] = (up_f * conv).astype(jnp.bfloat16)
    late_buf[0, 1] = dmixed.astype(jnp.bfloat16)
    late_copies = [make(late_buf.at[0], late_buf.at[k], "late", k - 1, line_peer(k)) for k in line_ways]
    start(late_copies)
    dz_buf[0, 0] = late_buf[0, 0]
    dz_buf[0, 1] = (dmixed * value_f).astype(jnp.bfloat16)
    dz_buf[0, 2] = (dmixed * key_f).astype(jnp.bfloat16)

    @pl.when(waits)
    def _():
        pl.semaphore_wait(sems["third"], 1)
        tuple_copy.start()

    arrive(w3_copies)
    start(w4_copies)

    def hand_out(way, index):
        return pltpu.make_async_remote_copy(
            src_ref=total_buf,
            dst_ref=total_buf,
            send_sem=sems["total_send"].at[index],
            recv_sem=sems["total_recv"].at[0],
            device_id=plane_peer(way),
            device_id_type=MESH,
        )

    total_copies = [hand_out(way, i) for i, way in enumerate(near_ways)]

    @pl.when(collects)
    def _():
        for a in range(na):
            arrived = make(tuple_buf.at[a], tuple_buf.at[a], "tuple", a, twin)
            pl.when(far != a)(arrived.wait_recv)
        whole_run = chained([piece(tuple_buf[a]) for a in range(na)], group_len)
        total_buf[...] = jnp.concatenate(whole_run[4:], axis=0)
        start(total_copies)

    arrive(kv_copies)
    arrive(w4_copies)
    arrive(late_copies)
    for k in line_ways:
        dmixed_k = late_buf[k, 1].astype(F32)
        dz_buf[k, 0] = late_buf[k, 0]
        dz_buf[k, 1] = (dmixed_k * raw_buf[k, 2].astype(F32)).astype(jnp.bfloat16)
        dz_buf[k, 2] = (dmixed_k * raw_buf[k, 1].astype(F32)).astype(jnp.bfloat16)
    rows = nzl * 3 * chans
    product = dot(
        dz_buf[...].reshape(rows, span), w_buf[...].reshape(rows, d_len), ((0,), (0,)), None
    )
    out_ref[...] = product.T.astype(jnp.bfloat16)

    pl.when(hands_on)(total_copies[0].wait_recv)
    total = total_buf[...]
    sums = dot_nt(
        lane_mode,
        jnp.concatenate([lane_chan * unfold(total[:blocks]), lane_chan * unfold(total[blocks:])], axis=0),
    )
    same, apart = sums[:, :chans], sums[:, chans:]
    scale = 1.0 / math.sqrt(float(token_count))
    gres_ref[...] = same * gain * scale
    glog_ref[...] = weight * (0.5 * same - rates * apart) * scale

    pl.when(core != 0)(wz_copies[0].wait_send)
    pl.when(hands_on)(tuple_copy.wait_send)

    @pl.when(collects)
    def _():
        for copy in total_copies:
            copy.wait_send()

    for copies in (
        plane_copies,
        near_copies,
        twin_copies,
        wz_copies[1:],
        kv_copies,
        late_copies,
        w2_copies,
        w3_copies,
        w4_copies,
    ):
        for copy in copies:
            copy.wait_send()


def finish(out_in, gres_in, glog_in, out_ref, gres_ref, glog_ref):
    out_ref[...] = out_in[...]
    gres_ref[...] = gres_in[...]
    glog_ref[...] = glog_in[...]


def per_device(dims, queries, keys, values, upstream, residues, rates, w_in):
    nx, nzh, ny, nco, nzl = dims
    nb, na = ny * nco, nx * nzh
    chans, span = queries.shape
    modes = residues.shape[1]
    d_len = w_in.shape[2] // nzl
    pairs = chans * modes
    blocks = pairs // LANES
    vmem = pl.BlockSpec(memory_space=pltpu.VMEM)
    counts = {
        "plane": nx * nb - 1,
        "near": nb - 1,
        "tuple": na,
        "total": nb - 1,
        "twin": 1,
        "wz": nzl // nco,
        "kv": nzl - 1,
        "late": nzl - 1,
        "w2": nx + ny - 2,
        "w3": nx // 2 * (ny - 1) + nx - 1,
        "w4": 1,
    }
    semaphores = {"load": 6, "own": 1}
    for name, count in counts.items():
        semaphores[name + "_send"] = count
        semaphores[name + "_recv"] = count
    arrays = [
        pltpu.with_memory_space_constraint(array, pltpu.HBM)
        for array in (queries, keys, values, upstream, residues.T, rates.T, w_in)
    ]
    results = pl.pallas_call(
        functools.partial(kernel, dims, span * na * nb, (*semaphores, "first", "second", "third")),
        out_shape=(
            jax.ShapeDtypeStruct((d_len, span), jnp.bfloat16),
            jax.ShapeDtypeStruct((modes, chans), F32),
            jax.ShapeDtypeStruct((modes, chans), F32),
        ),
        in_specs=[pl.BlockSpec(memory_space=pltpu.HBM)] * 7,
        out_specs=(vmem, vmem, vmem),
        scratch_shapes=[
            pltpu.VMEM((2, modes, chans), F32),
            pltpu.VMEM((nzl, 4, chans, span), jnp.bfloat16),
            pltpu.VMEM((nx * nb, 6 * blocks, LANES), F32),
            pltpu.VMEM((nzh, 2 * blocks, LANES), F32),
            pltpu.VMEM((na, 6 * blocks, LANES), F32),
            pltpu.VMEM((2 * blocks, LANES), F32),
            pltpu.VMEM((nzl, 2, chans, span), jnp.bfloat16),
            pltpu.VMEM((nzl, 3, chans, span), jnp.bfloat16),
            pltpu.VMEM((nzl, 3, chans, d_len), jnp.bfloat16),
        ]
        + [pltpu.SemaphoreType.DMA((count,)) for count in semaphores.values()]
        + [pltpu.SemaphoreType.REGULAR] * 3,
        compiler_params=pltpu.CompilerParams(
            collective_id=0, has_side_effects=True, vmem_limit_bytes=40 * 1024 * 1024
        ),
        cost_estimate=pl.CostEstimate(
            flops=2 * 3 * chans * nzl * d_len * span, bytes_accessed=2 * w_in.size, transcendentals=0
        ),
    )(*arrays)
    grad_input, grad_residues, grad_lograte = pl.pallas_call(
        finish,
        out_shape=(
            jax.ShapeDtypeStruct((d_len, span), jnp.bfloat16),
            jax.ShapeDtypeStruct((modes, chans), F32),
            jax.ShapeDtypeStruct((modes, chans), F32),
        ),
        in_specs=[vmem] * 3,
        out_specs=(vmem,) * 3,
        compiler_params=pltpu.CompilerParams(vmem_limit_bytes=4 * 1024 * 1024),
    )(*results)
    return grad_input, grad_residues.T, grad_lograte.T


def solution(mesh, dims=(4, 2, 4, 2, 8)):
    return jax.shard_map(
        functools.partial(per_device, dims),
        mesh=mesh,
        in_specs=(
            P("ch", "ctx"),
            P("ch", "ctx"),
            P("ch", "ctx"),
            P("ch", "ctx"),
            P("ch", None),
            P("ch", None),
            P(None, "ch", None),
        ),
        out_specs=(P("ch", "ctx"), P("ch", None), P("ch", None)),
        check_vma=False,
    )
```

```python
import functools
import math

import jax
import jax.numpy as jnp
from jax import lax
from jax.experimental import pallas as pl
from jax.experimental.pallas import tpu as pltpu
from jax.sharding import PartitionSpec as P

MESH = pl.DeviceIdType.MESH
HIGHEST = lax.Precision.HIGHEST
F32 = jnp.float32
LANES = 128
HALF = 16
CLOSE = 3


def dot(lhs, rhs, dims=((1,), (0,)), precision=HIGHEST):
    return lax.dot_general(
        lhs, rhs, (dims, ((), ())), precision=precision, preferred_element_type=F32
    )


def dot_nt(lhs, rhs):
    return dot(lhs, rhs, ((1,), (1,)))


def split(values):
    high = values.astype(jnp.bfloat16)
    return high, (values - high.astype(F32)).astype(jnp.bfloat16)


def dot_split(lhs, rhs, dims=((1,), (0,))):
    high, low = split(lhs)
    rows = lhs.shape[0]
    both = dot(jnp.concatenate([high, low], axis=0), rhs[0], dims, None)
    return both[:rows] + both[rows:] + dot(high, rhs[1], dims, None)


def iota(shape, dim):
    return lax.broadcasted_iota(jnp.int32, shape, dim)


def one_where(condition):
    return jnp.where(condition, 1.0, 0.0).astype(F32)


def chain(first, second, count, length, rate):
    s1, g1, sp1, gp1, a1, b1 = first
    s2, g2, sp2, gp2, a2, b2 = second
    step = jnp.exp(-float(length) * rate)
    whole = jnp.exp(-float(length * count) * rate)
    return (
        step * s1 + s2,
        g1 + whole * g2,
        step * (sp1 + float(length) * s1) + sp2,
        gp1 + whole * (gp2 + float(length * count) * g2),
        a1 + a2 + g2 * s1,
        b1 + b2 + gp2 * s1 + g2 * sp1,
    )


def kernel(dims, token_count, semaphores, *refs):
    nx, nzh, ny, nco, nzl = dims
    nb, na = ny * nco, nx * nzh
    q_hbm, k_hbm, v_hbm, u_hbm, res_hbm, rate_hbm, w_ref, out_ref, gres_ref, glog_ref = refs[:10]
    small_buf, raw_buf, half_buf, state_buf, tuple_buf, total_buf, late_buf, dz_buf, w_buf = refs[10:19]
    sems = dict(zip(semaphores, refs[19:]))
    ctx = lax.axis_index("ctx")
    zlo = lax.axis_index("ch")
    near = lax.rem(ctx, nb)
    far = ctx // nb
    core = lax.rem(ctx, nco)
    y = near // nco
    zh = lax.rem(far, nzh)
    x = far // nzh
    chans, span = raw_buf.shape[2:]
    modes = small_buf.shape[1]
    pairs = chans * modes
    blocks = pairs // LANES
    d_len = w_buf.shape[3]

    def ctx_of(px, pzh, py, pco):
        return ((px * nzh + pzh) * ny + py) * nco + pco

    def plane_peer(away):
        dx, dy, dc = away
        there = ctx_of(lax.rem(x + dx, nx), zh, lax.rem(y + dy, ny), lax.rem(core + dc, nco))
        return {"ctx": there, "ch": zlo}

    def line_peer(step):
        return {"ctx": ctx, "ch": lax.rem(zlo + step, nzl)}

    def x_peer(step):
        return {"ctx": ctx_of(lax.rem(x + step, nx), zh, y, core), "ch": zlo}

    def y_peer(step):
        return {"ctx": ctx_of(x, zh, lax.rem(y + step, ny), core), "ch": zlo}

    def by_distance(count):
        return sorted(range(count), key=lambda step: -min(step, count - step))

    def hops(away):
        return min(away[0], nx - away[0]) + min(away[1], ny - away[1])

    plane_ways = sorted(
        [(i, j, k) for i in range(nx) for j in range(ny) for k in range(nco)][1:],
        key=lambda away: -hops(away),
    )
    x_ways = [step for step in by_distance(nx) if step]
    y_ways = [step for step in by_distance(ny) if step]
    line_ways = list(range(1, nzl))
    sibling = plane_peer((0, 0, 1))
    near_ways = [way for way in plane_ways if way[0] == 0]
    twin = {"ctx": ctx_of(x, 1 - zh, y, core), "ch": zlo}

    def member(group):
        return {"ctx": group * nb + near, "ch": zlo}

    collects = near == far
    same_half = lax.rem(near, nzh) == zh
    opp_far = x * nzh + 1 - zh

    loads = [
        pltpu.make_async_copy(res_hbm, small_buf.at[0], sems["load"].at[4]),
        pltpu.make_async_copy(rate_hbm, small_buf.at[1], sems["load"].at[5]),
    ] + [
        pltpu.make_async_copy(ref, raw_buf.at[0, i], sems["load"].at[i])
        for i, ref in enumerate((q_hbm, k_hbm, v_hbm, u_hbm))
    ]
    for load in loads:
        load.start()

    barrier = pltpu.get_barrier_semaphore()

    def greet(semaphore, peer):
        pl.semaphore_signal(semaphore, inc=1, device_id=peer, device_id_type=MESH)

    def on_line(offset):
        return jnp.logical_and(zlo + offset >= 0, zlo + offset < nzl)

    def line_at(offset):
        return {"ctx": ctx, "ch": zlo + offset}

    def greet_line(semaphore, offsets, also=True):
        for offset in offsets:
            pl.when(jnp.logical_and(on_line(offset), also))(
                functools.partial(greet, semaphore, line_at(offset))
            )

    def count_line(offsets):
        return sum(on_line(offset).astype(jnp.int32) for offset in offsets)

    close = [sign * d for d in range(1, CLOSE + 1) for sign in (1, -1)]
    apart_ways = [sign * d for d in range(CLOSE + 1, nzl) for sign in (1, -1)]
    pl.when(zh == 0)(functools.partial(greet, barrier, twin))
    greet_line(barrier, close)
    greet_line(barrier, apart_ways, zh == 0)
    for way in plane_ways:
        greet(barrier, plane_peer(way))

    greeted = len(plane_ways) + jnp.where(zh == 0, nzl - 1, 1 + count_line(close))

    def make(src, dst, name, index, peer):
        return pltpu.make_async_remote_copy(
            src_ref=src,
            dst_ref=dst,
            send_sem=sems[name + "_send"].at[index],
            recv_sem=sems[name + "_recv"].at[index],
            device_id=peer,
            device_id_type=MESH,
        )

    def same_place(view, name, peer_of, ways, base=0):
        return [make(view, view, name, base + i, peer_of(way)) for i, way in enumerate(ways)]

    def start(copies):
        for copy in copies:
            copy.start()

    def arrive(copies):
        for copy in copies:
            copy.wait_recv()

    def folded(row):
        return [row[:, LANES * i : LANES * (i + 1)] for i in range(blocks)]

    def fold(row):
        return jnp.concatenate(folded(row), axis=0)

    def unfold(rows):
        return jnp.concatenate([rows[i : i + 1] for i in range(blocks)], axis=1)

    lane_mode = one_where(iota((modes, pairs), 0) == lax.rem(iota((modes, pairs), 1), modes))
    lane_chan = one_where(iota((chans, pairs), 0) == iota((chans, pairs), 1) // modes)
    time = iota((pairs, span), 1).astype(F32)
    upper = one_where(iota((span, span), 0) <= iota((span, span), 1)).astype(jnp.bfloat16)
    lower = one_where(iota((span, span), 0) >= iota((span, span), 1)).astype(jnp.bfloat16)

    def lane_sum(full):
        return jnp.sum(full * lane_chan, axis=0, keepdims=True)

    def diagonal_rows(full):
        return fold(lane_sum(full))

    def over_modes(values):
        return jnp.broadcast_to(values[:, None, :], (chans, modes, span)).reshape(pairs, span)

    def powers(rate_lane):
        high = rate_lane.astype(jnp.bfloat16).astype(F32)
        middle = (rate_lane - high).astype(jnp.bfloat16).astype(F32)
        parts = [high, middle, rate_lane - high - middle, jnp.zeros((HALF - 3, pairs), F32)]
        column = jnp.concatenate(parts, axis=0).astype(jnp.bfloat16)
        ones = jnp.ones((HALF, span), jnp.bfloat16)
        exponent = dot(column, ones, ((0,), (0,)), None) * time
        return jnp.exp(-exponent), jnp.exp(exponent)

    def sums_along(values, ones):
        high, low = split(values)
        return dot(high, ones, precision=None) + dot(low, ones, precision=None)

    nt = ((1,), (1,))

    loads[0].wait()
    loads[1].wait()
    rates = small_buf[1]
    gain = jnp.sqrt(2.0 * rates)
    weight = small_buf[0] * gain
    spread = dot(jnp.concatenate([rates, weight], axis=1), lane_mode, ((0,), (0,)))
    rate_lane = lane_sum(spread[:chans])
    weight_lane = lane_sum(spread[chans:])
    rate4, weight4 = fold(rate_lane), fold(weight_lane)
    falling, rising = powers(rate_lane)
    chunk_decay = jnp.exp(-float(span) * rate4)

    for load in loads[2:]:
        load.wait()
    query_f, key_f, value_f, up_f = (raw_buf[0, i].astype(F32) for i in range(4))
    mixed = key_f * value_f
    dgate = up_f * query_f
    falling_parts, rising_parts = split(falling), split(rising)
    s4 = diagonal_rows(dot_split(mixed, rising_parts, nt)) * chunk_decay
    g4 = diagonal_rows(dot_split(dgate, falling_parts, nt))
    here = x * nb + near
    first, rest = pl.ds(0, 2 * blocks), pl.ds(2 * blocks, 4 * blocks)
    half_buf[here, 0 : 2 * blocks] = jnp.concatenate([s4, g4], axis=0)

    pl.semaphore_wait(barrier, greeted)

    plane_copies = same_place(half_buf.at[here, first], "plane", plane_peer, plane_ways)

    start(plane_copies)

    @pl.when(zh == 1)
    def _():
        greet_line(sems["first"], (CLOSE, -CLOSE))

    per_core = nzl // nco
    half = x // (nx // 2)
    column = lax.rem(x, nx // 2) * ny + y

    def part_rows(rows_half):
        return pl.ds(pl.multiple_of(rows_half * HALF, HALF), HALF)

    def columns(begin, count):
        return pl.ds(pl.multiple_of(begin * LANES, LANES), count * LANES)

    def source_part(owner):
        return w_ref.at[:, part_rows(half), columns(owner * (d_len // LANES) + column, 1)]

    def part_of(slot):
        return w_buf.at[slot, :, part_rows(half), columns(column, 1)]

    own_part = pltpu.make_async_copy(source_part(zlo), part_of(0), sems["own"].at[0])
    wz_copies = []
    for i in range(per_core):
        slot = core * per_core + i
        peer = line_peer(slot)
        wz_copies.append(make(source_part(peer["ch"]), part_of(slot), "wz", i, peer))
    part = pl.ds(1, 2)
    kv_copies = [
        make(raw_buf.at[0, part], raw_buf.at[k, part], "kv", k - 1, line_peer(k)) for k in line_ways
    ]

    @pl.when(core == 0)
    def _():
        own_part.start()

    def start_line():
        pl.when(core != 0)(wz_copies[0].start)
        start(wz_copies[1:])

    pl.when(zh == 0)(start_line)

    mixed_rows = over_modes(mixed)
    forward = falling * sums_along(rising * mixed_rows, upper)
    backward = rising * sums_along(falling * over_modes(dgate), lower)
    forward_parts = split(forward)
    weight_diag = lane_chan * weight_lane
    conv = dot_split(weight_diag, forward_parts)
    dmixed = dot_split(weight_diag, split(backward))
    steps = iota((chans, span), 1).astype(F32)
    apart = split((forward - mixed_rows) * backward)
    ones = jnp.ones((HALF, span), jnp.bfloat16)
    apart_lane = (dot(ones, apart[0], nt, None) + dot(ones, apart[1], nt, None))[0:1]
    half_buf[here, 2 * blocks : 6 * blocks] = jnp.concatenate(
        [
            diagonal_rows(dot_split(mixed * (float(span) - steps), rising_parts, nt)) * chunk_decay,
            diagonal_rows(dot_split(dgate * steps, falling_parts, nt)),
            diagonal_rows(dot_split(dgate, forward_parts, nt)),
            fold(apart_lane),
        ],
        axis=0,
    )
    near_copies = same_place(half_buf.at[here, rest], "near", plane_peer, near_ways)
    start(near_copies)

    @pl.when(zh == 1)
    def _():
        pl.semaphore_wait(sems["first"], count_line((CLOSE, -CLOSE)))
        greet_line(sems["second"], (CLOSE + 1, -CLOSE - 1))

    rate8 = jnp.concatenate([rate4, rate4], axis=0)
    is_state = iota((2 * blocks, LANES), 0) < blocks

    def decay(length, if_state, if_other):
        away = jnp.where(is_state, if_state, if_other).astype(F32)
        power = jnp.exp(-float(length) * rate8 * jnp.maximum(away, 0.0))
        return jnp.where(away >= 0.0, power, 0.0)

    group_len = span * nb
    to_own, to_opp = [], []
    for px in range(nx):
        ahead = nzh * (x - px)
        to_own.append(decay(group_len, ahead - 1, -ahead - 1))
        to_opp.append(decay(group_len, ahead - 2 * zh, -ahead + 2 * zh - 2))
    inside = decay(span, near, nb - 1 - near)
    use = jnp.concatenate([weight4, weight4 * chunk_decay], axis=0)

    def group_states(px):
        run = jnp.zeros_like(rate4)
        back = run
        before = run
        after = run
        for i in range(nb):
            before = jnp.where(near == i, run, before)
            run = chunk_decay * run + half_buf[px * nb + i, 0:blocks]
            j = nb - 1 - i
            after = jnp.where(near == j, back, after)
            back = chunk_decay * back + half_buf[px * nb + j, blocks : 2 * blocks]
        return jnp.concatenate([before, after], axis=0), jnp.concatenate([run, back], axis=0)

    arrive(plane_copies)
    far_states = jnp.zeros_like(rate8)
    twin_states = jnp.zeros_like(rate8)
    from_near = jnp.zeros_like(rate8)
    for px in range(nx):
        around, states = group_states(px)
        from_near = jnp.where(x == px, around, from_near)
        far_states = far_states + to_own[px] * states
        twin_states = twin_states + to_opp[px] * states
    state_buf[zh] = twin_states
    twin_copies = [make(state_buf.at[zh], state_buf.at[zh], "twin", 0, twin)]

    @pl.when(zh == 1)
    def _():
        start(twin_copies)
        pl.semaphore_wait(sems["second"], count_line((CLOSE + 1, -CLOSE - 1)))
        start_line()

    def chained(pieces, length):
        total = pieces[0]
        for i in range(1, len(pieces)):
            total = chain(total, pieces[i], i, length, rate4)
        return total

    def piece(rows):
        return tuple(rows[j * blocks : (j + 1) * blocks] for j in range(6))

    arrive(near_copies)
    pieces = [piece(half_buf[x * nb + i]) for i in range(nb)]
    tuple_buf[far] = jnp.concatenate(chained(pieces, span), axis=0)
    target = {"ctx": jnp.where(same_half, member(near)["ctx"], twin["ctx"]), "ch": zlo}
    tuple_copy = make(tuple_buf.at[far], tuple_buf.at[far], "tuple", far, target)
    pass_copy = make(tuple_buf.at[opp_far], tuple_buf.at[opp_far], "tuple", opp_far, member(near))
    hands_on = jnp.logical_not(collects)
    passes = jnp.logical_and(same_half, hands_on)
    crosses = jnp.logical_not(same_half)
    pl.when(jnp.logical_or(passes, jnp.logical_and(crosses, zh == 1)))(tuple_copy.start)

    two = per_core // 2
    begin = core * per_core

    def across(slots, rows, cols):
        return w_buf.at[pl.ds(slots, two), :, rows, cols]

    x_peers = [(way, 0, 0) for way in x_ways]
    y_peers = [(0, way, 0) for way in y_ways]
    my_part = (part_rows(half), columns(column, 1))
    w2_copies = same_place(across(begin, *my_part), "w2", plane_peer, x_peers)
    w2_copies += same_place(across(begin + two, *my_part), "w2", plane_peer, y_peers, nx - 1)
    w3_copies = []
    for i in range(nx // 2):
        view = across(begin, pl.ds(0, 2 * HALF), columns(i * ny + y, 1))
        w3_copies += same_place(view, "w3", plane_peer, y_peers, i * (ny - 1))
    view = across(begin + two, part_rows(half), columns(lax.rem(x, nx // 2) * ny, ny))
    w3_copies += same_place(view, "w3", plane_peer, x_peers, nx // 2 * (ny - 1))
    whole = w_buf.at[pl.ds(begin, per_core)]
    w4_copies = [make(whole, whole, "w4", 0, sibling)]

    pl.when(core == 0)(own_part.wait)
    pl.when(core != 0)(wz_copies[0].wait_recv)
    arrive(wz_copies[1:])
    start(w2_copies)
    start(kv_copies)
    arrive(w2_copies)
    start(w3_copies)
    arrive(twin_copies)

    @pl.when(zh == 0)
    def _():
        start(twin_copies)

    states = use * (from_near + inside * (far_states + state_buf[1 - zh]))
    conv = conv + dot_split(lane_chan * unfold(states[:blocks]), falling_parts)
    dmixed = dmixed + dot_split(lane_chan * unfold(states[blocks:]), rising_parts)
    late_buf[0, 0] = (up_f * conv).astype(jnp.bfloat16)
    late_buf[0, 1] = dmixed.astype(jnp.bfloat16)
    late_copies = [make(late_buf.at[0], late_buf.at[k], "late", k - 1, line_peer(k)) for k in line_ways]
    start(late_copies)
    dz_buf[0, 0] = late_buf[0, 0]
    dz_buf[0, 1] = (dmixed * value_f).astype(jnp.bfloat16)
    dz_buf[0, 2] = (dmixed * key_f).astype(jnp.bfloat16)

    pl.when(jnp.logical_and(crosses, zh == 0))(tuple_copy.start)

    @pl.when(passes)
    def _():
        pass_copy.wait_recv()
        pass_copy.start()

    arrive(w3_copies)
    start(w4_copies)

    def hand_out(way, index):
        return pltpu.make_async_remote_copy(
            src_ref=total_buf,
            dst_ref=total_buf,
            send_sem=sems["total_send"].at[index],
            recv_sem=sems["total_recv"].at[0],
            device_id=plane_peer(way),
            device_id_type=MESH,
        )

    total_copies = [hand_out(way, i) for i, way in enumerate(near_ways)]

    @pl.when(collects)
    def _():
        for a in range(na):
            arrived = make(tuple_buf.at[a], tuple_buf.at[a], "tuple", a, twin)
            pl.when(far != a)(arrived.wait_recv)
        whole_run = chained([piece(tuple_buf[a]) for a in range(na)], group_len)
        total_buf[...] = jnp.concatenate(whole_run[4:], axis=0)
        start(total_copies)

    arrive(kv_copies)
    arrive(w4_copies)
    arrive(late_copies)
    for k in line_ways:
        dmixed_k = late_buf[k, 1].astype(F32)
        dz_buf[k, 0] = late_buf[k, 0]
        dz_buf[k, 1] = (dmixed_k * raw_buf[k, 2].astype(F32)).astype(jnp.bfloat16)
        dz_buf[k, 2] = (dmixed_k * raw_buf[k, 1].astype(F32)).astype(jnp.bfloat16)
    rows = nzl * 3 * chans
    product = dot(
        dz_buf[...].reshape(rows, span), w_buf[...].reshape(rows, d_len), ((0,), (0,)), None
    )
    out_ref[...] = product.T.astype(jnp.bfloat16)

    pl.when(hands_on)(total_copies[0].wait_recv)
    total = total_buf[...]
    sums = dot_nt(
        lane_mode,
        jnp.concatenate([lane_chan * unfold(total[:blocks]), lane_chan * unfold(total[blocks:])], axis=0),
    )
    same, apart = sums[:, :chans], sums[:, chans:]
    scale = 1.0 / math.sqrt(float(token_count))
    gres_ref[...] = same * gain * scale
    glog_ref[...] = weight * (0.5 * same - rates * apart) * scale

    pl.when(core != 0)(wz_copies[0].wait_send)
    pl.when(hands_on)(tuple_copy.wait_send)
    pl.when(passes)(pass_copy.wait_send)

    @pl.when(collects)
    def _():
        for copy in total_copies:
            copy.wait_send()

    for copies in (
        plane_copies,
        near_copies,
        twin_copies,
        wz_copies[1:],
        kv_copies,
        late_copies,
        w2_copies,
        w3_copies,
        w4_copies,
    ):
        for copy in copies:
            copy.wait_send()


def finish(out_in, gres_in, glog_in, out_ref, gres_ref, glog_ref):
    out_ref[...] = out_in[...]
    gres_ref[...] = gres_in[...]
    glog_ref[...] = glog_in[...]


def per_device(dims, queries, keys, values, upstream, residues, rates, w_in):
    nx, nzh, ny, nco, nzl = dims
    nb, na = ny * nco, nx * nzh
    chans, span = queries.shape
    modes = residues.shape[1]
    d_len = w_in.shape[2] // nzl
    pairs = chans * modes
    blocks = pairs // LANES
    vmem = pl.BlockSpec(memory_space=pltpu.VMEM)
    counts = {
        "plane": nx * nb - 1,
        "near": nb - 1,
        "tuple": na,
        "total": nb - 1,
        "twin": 1,
        "wz": nzl // nco,
        "kv": nzl - 1,
        "late": nzl - 1,
        "w2": nx + ny - 2,
        "w3": nx // 2 * (ny - 1) + nx - 1,
        "w4": 1,
    }
    semaphores = {"load": 6, "own": 1}
    for name, count in counts.items():
        semaphores[name + "_send"] = count
        semaphores[name + "_recv"] = count
    arrays = [
        pltpu.with_memory_space_constraint(array, pltpu.HBM)
        for array in (queries, keys, values, upstream, residues.T, rates.T, w_in)
    ]
    results = pl.pallas_call(
        functools.partial(kernel, dims, span * na * nb, (*semaphores, "first", "second")),
        out_shape=(
            jax.ShapeDtypeStruct((d_len, span), jnp.bfloat16),
            jax.ShapeDtypeStruct((modes, chans), F32),
            jax.ShapeDtypeStruct((modes, chans), F32),
        ),
        in_specs=[pl.BlockSpec(memory_space=pltpu.HBM)] * 7,
        out_specs=(vmem, vmem, vmem),
        scratch_shapes=[
            pltpu.VMEM((2, modes, chans), F32),
            pltpu.VMEM((nzl, 4, chans, span), jnp.bfloat16),
            pltpu.VMEM((nx * nb, 6 * blocks, LANES), F32),
            pltpu.VMEM((nzh, 2 * blocks, LANES), F32),
            pltpu.VMEM((na, 6 * blocks, LANES), F32),
            pltpu.VMEM((2 * blocks, LANES), F32),
            pltpu.VMEM((nzl, 2, chans, span), jnp.bfloat16),
            pltpu.VMEM((nzl, 3, chans, span), jnp.bfloat16),
            pltpu.VMEM((nzl, 3, chans, d_len), jnp.bfloat16),
        ]
        + [pltpu.SemaphoreType.DMA((count,)) for count in semaphores.values()]
        + [pltpu.SemaphoreType.REGULAR] * 2,
        compiler_params=pltpu.CompilerParams(
            collective_id=0, has_side_effects=True, vmem_limit_bytes=40 * 1024 * 1024
        ),
        cost_estimate=pl.CostEstimate(
            flops=2 * 3 * chans * nzl * d_len * span, bytes_accessed=2 * w_in.size, transcendentals=0
        ),
    )(*arrays)
    grad_input, grad_residues, grad_lograte = pl.pallas_call(
        finish,
        out_shape=(
            jax.ShapeDtypeStruct((d_len, span), jnp.bfloat16),
            jax.ShapeDtypeStruct((modes, chans), F32),
            jax.ShapeDtypeStruct((modes, chans), F32),
        ),
        in_specs=[vmem] * 3,
        out_specs=(vmem,) * 3,
        compiler_params=pltpu.CompilerParams(vmem_limit_bytes=4 * 1024 * 1024),
    )(*results)
    return grad_input, grad_residues.T, grad_lograte.T


def solution(mesh, dims=(4, 2, 4, 2, 8)):
    return jax.shard_map(
        functools.partial(per_device, dims),
        mesh=mesh,
        in_specs=(
            P("ch", "ctx"),
            P("ch", "ctx"),
            P("ch", "ctx"),
            P("ch", "ctx"),
            P("ch", None),
            P("ch", None),
            P(None, "ch", None),
        ),
        out_specs=(P("ch", "ctx"), P("ch", None), P("ch", None)),
        check_vma=False,
    )
```

```python
import functools
import math

import jax
import jax.numpy as jnp
from jax import lax
from jax.experimental import pallas as pl
from jax.experimental.pallas import tpu as pltpu
from jax.sharding import PartitionSpec as P

MESH = pl.DeviceIdType.MESH
HIGHEST = lax.Precision.HIGHEST
F32 = jnp.float32
LANES = 128
HALF = 16
CLOSE = 3


def dot(lhs, rhs, dims=((1,), (0,)), precision=HIGHEST):
    return lax.dot_general(
        lhs, rhs, (dims, ((), ())), precision=precision, preferred_element_type=F32
    )


def dot_nt(lhs, rhs):
    return dot(lhs, rhs, ((1,), (1,)))


def split(values):
    high = values.astype(jnp.bfloat16)
    return high, (values - high.astype(F32)).astype(jnp.bfloat16)


def dot_split(lhs, rhs, dims=((1,), (0,))):
    high, low = split(lhs)
    rows = lhs.shape[0]
    both = dot(jnp.concatenate([high, low], axis=0), rhs[0], dims, None)
    return both[:rows] + both[rows:] + dot(high, rhs[1], dims, None)


def iota(shape, dim):
    return lax.broadcasted_iota(jnp.int32, shape, dim)


def one_where(condition):
    return jnp.where(condition, 1.0, 0.0).astype(F32)


def chain(first, second, count, length, rate):
    s1, g1, sp1, gp1, a1, b1 = first
    s2, g2, sp2, gp2, a2, b2 = second
    step = jnp.exp(-float(length) * rate)
    whole = jnp.exp(-float(length * count) * rate)
    return (
        step * s1 + s2,
        g1 + whole * g2,
        step * (sp1 + float(length) * s1) + sp2,
        gp1 + whole * (gp2 + float(length * count) * g2),
        a1 + a2 + g2 * s1,
        b1 + b2 + gp2 * s1 + g2 * sp1,
    )


def kernel(dims, token_count, semaphores, *refs):
    nx, nzh, ny, nco, nzl = dims
    nb, na = ny * nco, nx * nzh
    q_hbm, k_hbm, v_hbm, u_hbm, res_hbm, rate_hbm, w_ref, out_ref, gres_ref, glog_ref = refs[:10]
    small_buf, raw_buf, half_buf, state_buf, tuple_buf, total_buf, late_buf, dz_buf, w_buf = refs[10:19]
    sems = dict(zip(semaphores, refs[19:]))
    ctx = lax.axis_index("ctx")
    zlo = lax.axis_index("ch")
    near = lax.rem(ctx, nb)
    far = ctx // nb
    core = lax.rem(ctx, nco)
    y = near // nco
    zh = lax.rem(far, nzh)
    x = far // nzh
    chans, span = raw_buf.shape[2:]
    modes = small_buf.shape[1]
    pairs = chans * modes
    blocks = pairs // LANES
    d_len = w_buf.shape[3]

    def ctx_of(px, pzh, py, pco):
        return ((px * nzh + pzh) * ny + py) * nco + pco

    def plane_peer(away):
        dx, dy, dc = away
        there = ctx_of(lax.rem(x + dx, nx), zh, lax.rem(y + dy, ny), lax.rem(core + dc, nco))
        return {"ctx": there, "ch": zlo}

    def line_peer(step):
        return {"ctx": ctx, "ch": lax.rem(zlo + step, nzl)}

    def x_peer(step):
        return {"ctx": ctx_of(lax.rem(x + step, nx), zh, y, core), "ch": zlo}

    def y_peer(step):
        return {"ctx": ctx_of(x, zh, lax.rem(y + step, ny), core), "ch": zlo}

    def by_distance(count):
        return sorted(range(count), key=lambda step: -min(step, count - step))

    def hops(away):
        return min(away[0], nx - away[0]) + min(away[1], ny - away[1])

    plane_ways = sorted(
        [(i, j, k) for i in range(nx) for j in range(ny) for k in range(nco)][1:],
        key=lambda away: -hops(away),
    )
    x_ways = [step for step in by_distance(nx) if step]
    y_ways = [step for step in by_distance(ny) if step]
    line_ways = list(range(1, nzl))
    sibling = plane_peer((0, 0, 1))
    near_ways = [way for way in plane_ways if way[0] == 0]
    twin = {"ctx": ctx_of(x, 1 - zh, y, core), "ch": zlo}

    def member(group):
        return {"ctx": group * nb + near, "ch": zlo}

    collects = near == far
    same_half = lax.rem(near, nzh) == zh
    opp_far = x * nzh + 1 - zh

    loads = [
        pltpu.make_async_copy(res_hbm, small_buf.at[0], sems["load"].at[4]),
        pltpu.make_async_copy(rate_hbm, small_buf.at[1], sems["load"].at[5]),
    ] + [
        pltpu.make_async_copy(ref, raw_buf.at[0, i], sems["load"].at[i])
        for i, ref in enumerate((q_hbm, k_hbm, v_hbm, u_hbm))
    ]
    for load in loads:
        load.start()

    barrier = pltpu.get_barrier_semaphore()

    def greet(semaphore, peer):
        pl.semaphore_signal(semaphore, inc=1, device_id=peer, device_id_type=MESH)

    def on_line(offset):
        return jnp.logical_and(zlo + offset >= 0, zlo + offset < nzl)

    def line_at(offset):
        return {"ctx": ctx, "ch": zlo + offset}

    def greet_line(semaphore, offsets, also=True):
        for offset in offsets:
            pl.when(jnp.logical_and(on_line(offset), also))(
                functools.partial(greet, semaphore, line_at(offset))
            )

    def count_line(offsets):
        return sum(on_line(offset).astype(jnp.int32) for offset in offsets)

    close = [sign * d for d in range(1, CLOSE + 1) for sign in (1, -1)]
    apart_ways = [sign * d for d in range(CLOSE + 1, nzl) for sign in (1, -1)]
    pl.when(zh == 0)(functools.partial(greet, barrier, twin))
    greet_line(barrier, close)
    greet_line(barrier, apart_ways, zh == 0)
    for way in plane_ways:
        greet(barrier, plane_peer(way))

    greeted = len(plane_ways) + jnp.where(zh == 0, nzl - 1, 1 + count_line(close))

    def make(src, dst, name, index, peer):
        return pltpu.make_async_remote_copy(
            src_ref=src,
            dst_ref=dst,
            send_sem=sems[name + "_send"].at[index],
            recv_sem=sems[name + "_recv"].at[index],
            device_id=peer,
            device_id_type=MESH,
        )

    def same_place(view, name, peer_of, ways, base=0):
        return [make(view, view, name, base + i, peer_of(way)) for i, way in enumerate(ways)]

    def start(copies):
        for copy in copies:
            copy.start()

    def arrive(copies):
        for copy in copies:
            copy.wait_recv()

    def folded(row):
        return [row[:, LANES * i : LANES * (i + 1)] for i in range(blocks)]

    def fold(row):
        return jnp.concatenate(folded(row), axis=0)

    def unfold(rows):
        return jnp.concatenate([rows[i : i + 1] for i in range(blocks)], axis=1)

    lane_mode = one_where(iota((modes, pairs), 0) == lax.rem(iota((modes, pairs), 1), modes))
    lane_chan = one_where(iota((chans, pairs), 0) == iota((chans, pairs), 1) // modes)
    time = iota((pairs, span), 1).astype(F32)
    upper = one_where(iota((span, span), 0) <= iota((span, span), 1)).astype(jnp.bfloat16)
    lower = one_where(iota((span, span), 0) >= iota((span, span), 1)).astype(jnp.bfloat16)

    def lane_sum(full):
        return jnp.sum(full * lane_chan, axis=0, keepdims=True)

    def diagonal_rows(full):
        return fold(lane_sum(full))

    def over_modes(values):
        return jnp.broadcast_to(values[:, None, :], (chans, modes, span)).reshape(pairs, span)

    def powers(rate_lane):
        high = rate_lane.astype(jnp.bfloat16).astype(F32)
        middle = (rate_lane - high).astype(jnp.bfloat16).astype(F32)
        parts = [high, middle, rate_lane - high - middle, jnp.zeros((HALF - 3, pairs), F32)]
        column = jnp.concatenate(parts, axis=0).astype(jnp.bfloat16)
        ones = jnp.ones((HALF, span), jnp.bfloat16)
        exponent = dot(column, ones, ((0,), (0,)), None) * time
        return jnp.exp(-exponent), jnp.exp(exponent)

    def sums_along(values, ones):
        high, low = split(values)
        return dot(high, ones, precision=None) + dot(low, ones, precision=None)

    nt = ((1,), (1,))

    loads[0].wait()
    loads[1].wait()
    rates = small_buf[1]
    gain = jnp.sqrt(2.0 * rates)
    weight = small_buf[0] * gain
    spread = dot(jnp.concatenate([rates, weight], axis=1), lane_mode, ((0,), (0,)))
    rate_lane = lane_sum(spread[:chans])
    weight_lane = lane_sum(spread[chans:])
    rate4, weight4 = fold(rate_lane), fold(weight_lane)
    falling, rising = powers(rate_lane)
    chunk_decay = jnp.exp(-float(span) * rate4)

    for load in loads[2:]:
        load.wait()
    query_f, key_f, value_f, up_f = (raw_buf[0, i].astype(F32) for i in range(4))
    mixed = key_f * value_f
    dgate = up_f * query_f
    falling_parts, rising_parts = split(falling), split(rising)
    s4 = diagonal_rows(dot_split(mixed, rising_parts, nt)) * chunk_decay
    g4 = diagonal_rows(dot_split(dgate, falling_parts, nt))
    here = x * nb + near
    first, rest = pl.ds(0, 2 * blocks), pl.ds(2 * blocks, 4 * blocks)
    half_buf[here, 0 : 2 * blocks] = jnp.concatenate([s4, g4], axis=0)

    pl.semaphore_wait(barrier, greeted)

    plane_copies = same_place(half_buf.at[here, first], "plane", plane_peer, plane_ways)

    start(plane_copies)

    @pl.when(zh == 1)
    def _():
        greet_line(sems["first"], (CLOSE, -CLOSE))

    per_core = nzl // nco
    half = x // (nx // 2)
    column = lax.rem(x, nx // 2) * ny + y

    def part_rows(rows_half):
        return pl.ds(pl.multiple_of(rows_half * HALF, HALF), HALF)

    def columns(begin, count):
        return pl.ds(pl.multiple_of(begin * LANES, LANES), count * LANES)

    def source_part(owner):
        return w_ref.at[:, part_rows(half), columns(owner * (d_len // LANES) + column, 1)]

    def part_of(slot):
        return w_buf.at[slot, :, part_rows(half), columns(column, 1)]

    own_part = pltpu.make_async_copy(source_part(zlo), part_of(0), sems["own"].at[0])
    wz_copies = []
    for i in range(per_core):
        slot = core * per_core + i
        peer = line_peer(slot)
        wz_copies.append(make(source_part(peer["ch"]), part_of(slot), "wz", i, peer))
    part = pl.ds(1, 2)
    kv_copies = [
        make(raw_buf.at[0, part], raw_buf.at[k, part], "kv", k - 1, line_peer(k)) for k in line_ways
    ]

    @pl.when(core == 0)
    def _():
        own_part.start()

    def start_line():
        pl.when(core != 0)(wz_copies[0].start)
        start(wz_copies[1:])

    pl.when(zh == 0)(start_line)

    mixed_rows = over_modes(mixed)
    forward = falling * sums_along(rising * mixed_rows, upper)
    backward = rising * sums_along(falling * over_modes(dgate), lower)
    forward_parts = split(forward)
    weight_diag = lane_chan * weight_lane
    conv = dot_split(weight_diag, forward_parts)
    dmixed = dot_split(weight_diag, split(backward))
    steps = iota((chans, span), 1).astype(F32)
    apart = split((forward - mixed_rows) * backward)
    ones = jnp.ones((HALF, span), jnp.bfloat16)
    apart_lane = (dot(ones, apart[0], nt, None) + dot(ones, apart[1], nt, None))[0:1]
    half_buf[here, 2 * blocks : 6 * blocks] = jnp.concatenate(
        [
            diagonal_rows(dot_split(mixed * (float(span) - steps), rising_parts, nt)) * chunk_decay,
            diagonal_rows(dot_split(dgate * steps, falling_parts, nt)),
            diagonal_rows(dot_split(dgate, forward_parts, nt)),
            fold(apart_lane),
        ],
        axis=0,
    )
    near_copies = same_place(half_buf.at[here, rest], "near", plane_peer, near_ways)
    start(near_copies)

    @pl.when(zh == 1)
    def _():
        pl.semaphore_wait(sems["first"], count_line((CLOSE, -CLOSE)))
        greet_line(sems["second"], (CLOSE + 1, -CLOSE - 1))

    rate8 = jnp.concatenate([rate4, rate4], axis=0)
    is_state = iota((2 * blocks, LANES), 0) < blocks

    def decay(length, if_state, if_other):
        away = jnp.where(is_state, if_state, if_other).astype(F32)
        power = jnp.exp(-float(length) * rate8 * jnp.maximum(away, 0.0))
        return jnp.where(away >= 0.0, power, 0.0)

    group_len = span * nb
    to_own, to_opp = [], []
    for px in range(nx):
        ahead = nzh * (x - px)
        to_own.append(decay(group_len, ahead - 1, -ahead - 1))
        to_opp.append(decay(group_len, ahead - 2 * zh, -ahead + 2 * zh - 2))
    inside = decay(span, near, nb - 1 - near)
    use = jnp.concatenate([weight4, weight4 * chunk_decay], axis=0)

    def group_states(px):
        run = jnp.zeros_like(rate4)
        back = run
        before = run
        after = run
        for i in range(nb):
            before = jnp.where(near == i, run, before)
            run = chunk_decay * run + half_buf[px * nb + i, 0:blocks]
            j = nb - 1 - i
            after = jnp.where(near == j, back, after)
            back = chunk_decay * back + half_buf[px * nb + j, blocks : 2 * blocks]
        return jnp.concatenate([before, after], axis=0), jnp.concatenate([run, back], axis=0)

    arrive(plane_copies)
    far_states = jnp.zeros_like(rate8)
    twin_states = jnp.zeros_like(rate8)
    from_near = jnp.zeros_like(rate8)
    for px in range(nx):
        around, states = group_states(px)
        from_near = jnp.where(x == px, around, from_near)
        far_states = far_states + to_own[px] * states
        twin_states = twin_states + to_opp[px] * states
    state_buf[zh] = twin_states
    twin_copies = [make(state_buf.at[zh], state_buf.at[zh], "twin", 0, twin)]

    @pl.when(zh == 1)
    def _():
        start(twin_copies)

    def chained(pieces, length):
        total = pieces[0]
        for i in range(1, len(pieces)):
            total = chain(total, pieces[i], i, length, rate4)
        return total

    def piece(rows):
        return tuple(rows[j * blocks : (j + 1) * blocks] for j in range(6))

    arrive(near_copies)
    pieces = [piece(half_buf[x * nb + i]) for i in range(nb)]
    tuple_buf[far] = jnp.concatenate(chained(pieces, span), axis=0)
    target = {"ctx": jnp.where(same_half, member(near)["ctx"], twin["ctx"]), "ch": zlo}
    tuple_copy = make(tuple_buf.at[far], tuple_buf.at[far], "tuple", far, target)
    pass_copy = make(tuple_buf.at[opp_far], tuple_buf.at[opp_far], "tuple", opp_far, member(near))
    hands_on = jnp.logical_not(collects)
    passes = jnp.logical_and(same_half, hands_on)
    crosses = jnp.logical_not(same_half)
    pl.when(jnp.logical_or(passes, jnp.logical_and(crosses, zh == 1)))(tuple_copy.start)

    @pl.when(zh == 1)
    def _():
        pl.semaphore_wait(sems["second"], count_line((CLOSE + 1, -CLOSE - 1)))
        start_line()

    two = per_core // 2
    begin = core * per_core

    def across(slots, rows, cols):
        return w_buf.at[pl.ds(slots, two), :, rows, cols]

    x_peers = [(way, 0, 0) for way in x_ways]
    y_peers = [(0, way, 0) for way in y_ways]
    my_part = (part_rows(half), columns(column, 1))
    w2_copies = same_place(across(begin, *my_part), "w2", plane_peer, x_peers)
    w2_copies += same_place(across(begin + two, *my_part), "w2", plane_peer, y_peers, nx - 1)
    w3_copies = []
    for i in range(nx // 2):
        view = across(begin, pl.ds(0, 2 * HALF), columns(i * ny + y, 1))
        w3_copies += same_place(view, "w3", plane_peer, y_peers, i * (ny - 1))
    view = across(begin + two, part_rows(half), columns(lax.rem(x, nx // 2) * ny, ny))
    w3_copies += same_place(view, "w3", plane_peer, x_peers, nx // 2 * (ny - 1))
    w4_copies = []

    def hand_over(view):
        w4_copies.append(make(view, view, "w4", len(w4_copies), sibling))
        w4_copies[-1].start()

    def column_from(py, i):
        return across(begin, pl.ds(0, 2 * HALF), columns(i * ny + py, 1))

    def rows_from(px):
        return across(begin + two, part_rows(px // (nx // 2)), columns(lax.rem(px, nx // 2) * ny, ny))

    pl.when(core == 0)(own_part.wait)
    pl.when(core != 0)(wz_copies[0].wait_recv)
    arrive(wz_copies[1:])
    start(w2_copies)
    start(kv_copies)
    arrive(w2_copies)
    start(w3_copies)
    for i in range(nx // 2):
        hand_over(column_from(y, i))
    hand_over(rows_from(x))
    arrive(twin_copies)

    @pl.when(zh == 0)
    def _():
        start(twin_copies)

    states = use * (from_near + inside * (far_states + state_buf[1 - zh]))
    conv = conv + dot_split(lane_chan * unfold(states[:blocks]), falling_parts)
    dmixed = dmixed + dot_split(lane_chan * unfold(states[blocks:]), rising_parts)
    late_buf[0, 0] = (up_f * conv).astype(jnp.bfloat16)
    late_buf[0, 1] = dmixed.astype(jnp.bfloat16)
    late_copies = [make(late_buf.at[0], late_buf.at[k], "late", k - 1, line_peer(k)) for k in line_ways]

    @pl.when(zlo < nzl // 2)
    def _():
        start(reversed(late_copies))

    @pl.when(zlo >= nzl // 2)
    def _():
        start(late_copies)

    dz_buf[0, 0] = late_buf[0, 0]
    dz_buf[0, 1] = (dmixed * value_f).astype(jnp.bfloat16)
    dz_buf[0, 2] = (dmixed * key_f).astype(jnp.bfloat16)

    pl.when(jnp.logical_and(crosses, zh == 0))(tuple_copy.start)

    @pl.when(passes)
    def _():
        pass_copy.wait_recv()
        pass_copy.start()

    for index, way in reversed(list(enumerate(y_ways))):
        for i in range(nx // 2):
            w3_copies[i * (ny - 1) + index].wait_recv()
            hand_over(column_from(lax.rem(y - way + ny, ny), i))
    for index, way in reversed(list(enumerate(x_ways))):
        w3_copies[nx // 2 * (ny - 1) + index].wait_recv()
        hand_over(rows_from(lax.rem(x - way + nx, nx)))

    def hand_out(way, index):
        return pltpu.make_async_remote_copy(
            src_ref=total_buf,
            dst_ref=total_buf,
            send_sem=sems["total_send"].at[index],
            recv_sem=sems["total_recv"].at[0],
            device_id=plane_peer(way),
            device_id_type=MESH,
        )

    total_copies = [hand_out(way, i) for i, way in enumerate(near_ways)]

    @pl.when(collects)
    def _():
        for a in range(na):
            arrived = make(tuple_buf.at[a], tuple_buf.at[a], "tuple", a, twin)
            pl.when(far != a)(arrived.wait_recv)
        whole_run = chained([piece(tuple_buf[a]) for a in range(na)], group_len)
        total_buf[...] = jnp.concatenate(whole_run[4:], axis=0)
        start(total_copies)

    arrive(kv_copies)
    arrive(w4_copies)
    for k in line_ways:
        late_copies[k - 1].wait_recv()
        dmixed_k = late_buf[k, 1].astype(F32)
        dz_buf[k, 0] = late_buf[k, 0]
        dz_buf[k, 1] = (dmixed_k * raw_buf[k, 2].astype(F32)).astype(jnp.bfloat16)
        dz_buf[k, 2] = (dmixed_k * raw_buf[k, 1].astype(F32)).astype(jnp.bfloat16)
    rows = nzl * 3 * chans
    product = dot(
        dz_buf[...].reshape(rows, span), w_buf[...].reshape(rows, d_len), ((0,), (0,)), None
    )
    out_ref[...] = product.T.astype(jnp.bfloat16)

    pl.when(hands_on)(total_copies[0].wait_recv)
    total = total_buf[...]
    sums = dot_nt(
        lane_mode,
        jnp.concatenate([lane_chan * unfold(total[:blocks]), lane_chan * unfold(total[blocks:])], axis=0),
    )
    same, apart = sums[:, :chans], sums[:, chans:]
    scale = 1.0 / math.sqrt(float(token_count))
    gres_ref[...] = same * gain * scale
    glog_ref[...] = weight * (0.5 * same - rates * apart) * scale

    pl.when(core != 0)(wz_copies[0].wait_send)
    pl.when(hands_on)(tuple_copy.wait_send)
    pl.when(passes)(pass_copy.wait_send)

    @pl.when(collects)
    def _():
        for copy in total_copies:
            copy.wait_send()

    for copies in (
        plane_copies,
        near_copies,
        twin_copies,
        wz_copies[1:],
        kv_copies,
        late_copies,
        w2_copies,
        w3_copies,
        w4_copies,
    ):
        for copy in copies:
            copy.wait_send()


def finish(out_in, gres_in, glog_in, out_ref, gres_ref, glog_ref):
    out_ref[...] = out_in[...]
    gres_ref[...] = gres_in[...]
    glog_ref[...] = glog_in[...]


def per_device(dims, queries, keys, values, upstream, residues, rates, w_in):
    nx, nzh, ny, nco, nzl = dims
    nb, na = ny * nco, nx * nzh
    chans, span = queries.shape
    modes = residues.shape[1]
    d_len = w_in.shape[2] // nzl
    pairs = chans * modes
    blocks = pairs // LANES
    vmem = pl.BlockSpec(memory_space=pltpu.VMEM)
    counts = {
        "plane": nx * nb - 1,
        "near": nb - 1,
        "tuple": na,
        "total": nb - 1,
        "twin": 1,
        "wz": nzl // nco,
        "kv": nzl - 1,
        "late": nzl - 1,
        "w2": nx + ny - 2,
        "w3": nx // 2 * (ny - 1) + nx - 1,
        "w4": nx // 2 * ny + nx,
    }
    semaphores = {"load": 6, "own": 1}
    for name, count in counts.items():
        semaphores[name + "_send"] = count
        semaphores[name + "_recv"] = count
    arrays = [
        pltpu.with_memory_space_constraint(array, pltpu.HBM)
        for array in (queries, keys, values, upstream, residues.T, rates.T, w_in)
    ]
    results = pl.pallas_call(
        functools.partial(kernel, dims, span * na * nb, (*semaphores, "first", "second")),
        out_shape=(
            jax.ShapeDtypeStruct((d_len, span), jnp.bfloat16),
            jax.ShapeDtypeStruct((modes, chans), F32),
            jax.ShapeDtypeStruct((modes, chans), F32),
        ),
        in_specs=[pl.BlockSpec(memory_space=pltpu.HBM)] * 7,
        out_specs=(vmem, vmem, vmem),
        scratch_shapes=[
            pltpu.VMEM((2, modes, chans), F32),
            pltpu.VMEM((nzl, 4, chans, span), jnp.bfloat16),
            pltpu.VMEM((nx * nb, 6 * blocks, LANES), F32),
            pltpu.VMEM((nzh, 2 * blocks, LANES), F32),
            pltpu.VMEM((na, 6 * blocks, LANES), F32),
            pltpu.VMEM((2 * blocks, LANES), F32),
            pltpu.VMEM((nzl, 2, chans, span), jnp.bfloat16),
            pltpu.VMEM((nzl, 3, chans, span), jnp.bfloat16),
            pltpu.VMEM((nzl, 3, chans, d_len), jnp.bfloat16),
        ]
        + [pltpu.SemaphoreType.DMA((count,)) for count in semaphores.values()]
        + [pltpu.SemaphoreType.REGULAR] * 2,
        compiler_params=pltpu.CompilerParams(
            collective_id=0, has_side_effects=True, vmem_limit_bytes=40 * 1024 * 1024
        ),
        cost_estimate=pl.CostEstimate(
            flops=2 * 3 * chans * nzl * d_len * span, bytes_accessed=2 * w_in.size, transcendentals=0
        ),
    )(*arrays)
    grad_input, grad_residues, grad_lograte = pl.pallas_call(
        finish,
        out_shape=(
            jax.ShapeDtypeStruct((d_len, span), jnp.bfloat16),
            jax.ShapeDtypeStruct((modes, chans), F32),
            jax.ShapeDtypeStruct((modes, chans), F32),
        ),
        in_specs=[vmem] * 3,
        out_specs=(vmem,) * 3,
        compiler_params=pltpu.CompilerParams(vmem_limit_bytes=4 * 1024 * 1024),
    )(*results)
    return grad_input, grad_residues.T, grad_lograte.T


def solution(mesh, dims=(4, 2, 4, 2, 8)):
    return jax.shard_map(
        functools.partial(per_device, dims),
        mesh=mesh,
        in_specs=(
            P("ch", "ctx"),
            P("ch", "ctx"),
            P("ch", "ctx"),
            P("ch", "ctx"),
            P("ch", None),
            P("ch", None),
            P(None, "ch", None),
        ),
        out_specs=(P("ch", "ctx"), P("ch", None), P("ch", None)),
        check_vma=False,
    )
```

```python
import functools
import math

import jax
import jax.numpy as jnp
from jax import lax
from jax.experimental import pallas as pl
from jax.experimental.pallas import tpu as pltpu
from jax.sharding import PartitionSpec as P

MESH = pl.DeviceIdType.MESH
HIGHEST = lax.Precision.HIGHEST
F32 = jnp.float32
LANES = 128
HALF = 16
CLOSE = 3


def dot(lhs, rhs, dims=((1,), (0,)), precision=HIGHEST):
    return lax.dot_general(
        lhs, rhs, (dims, ((), ())), precision=precision, preferred_element_type=F32
    )


def dot_nt(lhs, rhs):
    return dot(lhs, rhs, ((1,), (1,)))


def split(values):
    high = values.astype(jnp.bfloat16)
    return high, (values - high.astype(F32)).astype(jnp.bfloat16)


def dot_split(lhs, rhs, dims=((1,), (0,))):
    high, low = split(lhs)
    rows = lhs.shape[0]
    both = dot(jnp.concatenate([high, low], axis=0), rhs[0], dims, None)
    return both[:rows] + both[rows:] + dot(high, rhs[1], dims, None)


def iota(shape, dim):
    return lax.broadcasted_iota(jnp.int32, shape, dim)


def one_where(condition):
    return jnp.where(condition, 1.0, 0.0).astype(F32)


def chain(first, second, count, length, rate):
    s1, g1, sp1, gp1, a1, b1 = first
    s2, g2, sp2, gp2, a2, b2 = second
    step = jnp.exp(-float(length) * rate)
    whole = jnp.exp(-float(length * count) * rate)
    return (
        step * s1 + s2,
        g1 + whole * g2,
        step * (sp1 + float(length) * s1) + sp2,
        gp1 + whole * (gp2 + float(length * count) * g2),
        a1 + a2 + g2 * s1,
        b1 + b2 + gp2 * s1 + g2 * sp1,
    )


def kernel(dims, token_count, semaphores, *refs):
    nx, nzh, ny, nco, nzl = dims
    nb, na = ny * nco, nx * nzh
    q_hbm, k_hbm, v_hbm, u_hbm, res_hbm, rate_hbm, w_ref, out_ref, gres_ref, glog_ref = refs[:10]
    small_buf, raw_buf, half_buf, state_buf, tuple_buf, total_buf, late_buf, dz_buf, w_buf = refs[10:19]
    sems = dict(zip(semaphores, refs[19:]))
    ctx = lax.axis_index("ctx")
    zlo = lax.axis_index("ch")
    near = lax.rem(ctx, nb)
    far = ctx // nb
    core = lax.rem(ctx, nco)
    y = near // nco
    zh = lax.rem(far, nzh)
    x = far // nzh
    chans, span = raw_buf.shape[2:]
    modes = small_buf.shape[1]
    pairs = chans * modes
    blocks = pairs // LANES
    d_len = w_buf.shape[3]

    def ctx_of(px, pzh, py, pco):
        return ((px * nzh + pzh) * ny + py) * nco + pco

    def plane_peer(away):
        dx, dy, dc = away
        there = ctx_of(lax.rem(x + dx, nx), zh, lax.rem(y + dy, ny), lax.rem(core + dc, nco))
        return {"ctx": there, "ch": zlo}

    def line_peer(step):
        return {"ctx": ctx, "ch": lax.rem(zlo + step, nzl)}

    def x_peer(step):
        return {"ctx": ctx_of(lax.rem(x + step, nx), zh, y, core), "ch": zlo}

    def y_peer(step):
        return {"ctx": ctx_of(x, zh, lax.rem(y + step, ny), core), "ch": zlo}

    def by_distance(count):
        return sorted(range(count), key=lambda step: -min(step, count - step))

    def hops(away):
        return min(away[0], nx - away[0]) + min(away[1], ny - away[1])

    plane_ways = sorted(
        [(i, j, k) for i in range(nx) for j in range(ny) for k in range(nco)][1:],
        key=lambda away: -hops(away),
    )
    x_ways = [step for step in by_distance(nx) if step]
    y_ways = [step for step in by_distance(ny) if step]
    line_ways = list(range(1, nzl))
    sibling = plane_peer((0, 0, 1))
    near_ways = [way for way in plane_ways if way[0] == 0]
    twin = {"ctx": ctx_of(x, 1 - zh, y, core), "ch": zlo}

    def member(group):
        return {"ctx": group * nb + near, "ch": zlo}

    collects = near == far
    same_half = lax.rem(near, nzh) == zh
    opp_far = x * nzh + 1 - zh

    loads = [
        pltpu.make_async_copy(res_hbm, small_buf.at[0], sems["load"].at[4]),
        pltpu.make_async_copy(rate_hbm, small_buf.at[1], sems["load"].at[5]),
    ] + [
        pltpu.make_async_copy(ref, raw_buf.at[0, i], sems["load"].at[i])
        for i, ref in enumerate((q_hbm, k_hbm, v_hbm, u_hbm))
    ]
    for load in loads:
        load.start()

    barrier = pltpu.get_barrier_semaphore()

    def greet(semaphore, peer):
        pl.semaphore_signal(semaphore, inc=1, device_id=peer, device_id_type=MESH)

    def on_line(offset):
        return jnp.logical_and(zlo + offset >= 0, zlo + offset < nzl)

    def line_at(offset):
        return {"ctx": ctx, "ch": zlo + offset}

    def greet_line(semaphore, offsets, also=True):
        for offset in offsets:
            pl.when(jnp.logical_and(on_line(offset), also))(
                functools.partial(greet, semaphore, line_at(offset))
            )

    def count_line(offsets):
        return sum(on_line(offset).astype(jnp.int32) for offset in offsets)

    close = [sign * d for d in range(1, CLOSE + 1) for sign in (1, -1)]
    apart_ways = [sign * d for d in range(CLOSE + 1, nzl) for sign in (1, -1)]
    pl.when(zh == 0)(functools.partial(greet, barrier, twin))
    greet_line(barrier, close)
    greet_line(barrier, apart_ways, zh == 0)
    for way in plane_ways:
        greet(barrier, plane_peer(way))

    greeted = len(plane_ways) + jnp.where(zh == 0, nzl - 1, 1 + count_line(close))

    def make(src, dst, name, index, peer):
        return pltpu.make_async_remote_copy(
            src_ref=src,
            dst_ref=dst,
            send_sem=sems[name + "_send"].at[index],
            recv_sem=sems[name + "_recv"].at[index],
            device_id=peer,
            device_id_type=MESH,
        )

    def same_place(view, name, peer_of, ways, base=0):
        return [make(view, view, name, base + i, peer_of(way)) for i, way in enumerate(ways)]

    def start(copies):
        for copy in copies:
            copy.start()

    def arrive(copies):
        for copy in copies:
            copy.wait_recv()

    def folded(row):
        return [row[:, LANES * i : LANES * (i + 1)] for i in range(blocks)]

    def fold(row):
        return jnp.concatenate(folded(row), axis=0)

    def unfold(rows):
        return jnp.concatenate([rows[i : i + 1] for i in range(blocks)], axis=1)

    lane_mode = one_where(iota((modes, pairs), 0) == lax.rem(iota((modes, pairs), 1), modes))
    lane_chan = one_where(iota((chans, pairs), 0) == iota((chans, pairs), 1) // modes)
    time = iota((pairs, span), 1).astype(F32)
    upper = one_where(iota((span, span), 0) <= iota((span, span), 1)).astype(jnp.bfloat16)
    lower = one_where(iota((span, span), 0) >= iota((span, span), 1)).astype(jnp.bfloat16)

    def lane_sum(full):
        return jnp.sum(full * lane_chan, axis=0, keepdims=True)

    def diagonal_rows(full):
        return fold(lane_sum(full))

    def over_modes(values):
        return jnp.broadcast_to(values[:, None, :], (chans, modes, span)).reshape(pairs, span)

    def powers(rate_lane):
        high = rate_lane.astype(jnp.bfloat16).astype(F32)
        middle = (rate_lane - high).astype(jnp.bfloat16).astype(F32)
        parts = [high, middle, rate_lane - high - middle, jnp.zeros((HALF - 3, pairs), F32)]
        column = jnp.concatenate(parts, axis=0).astype(jnp.bfloat16)
        ones = jnp.ones((HALF, span), jnp.bfloat16)
        exponent = dot(column, ones, ((0,), (0,)), None) * time
        return jnp.exp(-exponent), jnp.exp(exponent)

    def sums_along(values, ones):
        high, low = split(values)
        return dot(high, ones, precision=None) + dot(low, ones, precision=None)

    nt = ((1,), (1,))

    loads[0].wait()
    loads[1].wait()
    rates = small_buf[1]
    gain = jnp.sqrt(2.0 * rates)
    weight = small_buf[0] * gain
    spread = dot(jnp.concatenate([rates, weight], axis=1), lane_mode, ((0,), (0,)))
    rate_lane = lane_sum(spread[:chans])
    weight_lane = lane_sum(spread[chans:])
    rate4, weight4 = fold(rate_lane), fold(weight_lane)
    falling, rising = powers(rate_lane)
    chunk_decay = jnp.exp(-float(span) * rate4)

    for load in loads[2:]:
        load.wait()
    query_f, key_f, value_f, up_f = (raw_buf[0, i].astype(F32) for i in range(4))
    mixed = key_f * value_f
    dgate = up_f * query_f
    falling_parts, rising_parts = split(falling), split(rising)
    s4 = diagonal_rows(dot_split(mixed, rising_parts, nt)) * chunk_decay
    g4 = diagonal_rows(dot_split(dgate, falling_parts, nt))
    here = x * nb + near
    first, rest = pl.ds(0, 2 * blocks), pl.ds(2 * blocks, 4 * blocks)
    half_buf[here, 0 : 2 * blocks] = jnp.concatenate([s4, g4], axis=0)

    pl.semaphore_wait(barrier, greeted)

    plane_copies = same_place(half_buf.at[here, first], "plane", plane_peer, plane_ways)

    start(plane_copies)

    @pl.when(zh == 1)
    def _():
        greet_line(sems["first"], (CLOSE, -CLOSE))

    per_core = nzl // nco
    half = x // (nx // 2)
    column = lax.rem(x, nx // 2) * ny + y

    def part_rows(rows_half):
        return pl.ds(pl.multiple_of(rows_half * HALF, HALF), HALF)

    def columns(begin, count):
        return pl.ds(pl.multiple_of(begin * LANES, LANES), count * LANES)

    def source_part(owner):
        return w_ref.at[:, part_rows(half), columns(owner * (d_len // LANES) + column, 1)]

    def part_of(slot):
        return w_buf.at[slot, :, part_rows(half), columns(column, 1)]

    own_part = pltpu.make_async_copy(source_part(zlo), part_of(0), sems["own"].at[0])
    wz_copies = []
    for i in range(per_core):
        slot = core * per_core + i
        peer = line_peer(slot)
        wz_copies.append(make(source_part(peer["ch"]), part_of(slot), "wz", i, peer))
    part = pl.ds(1, 2)
    kv_copies = [
        make(raw_buf.at[0, part], raw_buf.at[k, part], "kv", k - 1, line_peer(k)) for k in line_ways
    ]

    @pl.when(core == 0)
    def _():
        own_part.start()

    def start_line():
        pl.when(core != 0)(wz_copies[0].start)
        start(wz_copies[1:])

    pl.when(zh == 0)(start_line)

    mixed_rows = over_modes(mixed)
    forward = falling * sums_along(rising * mixed_rows, upper)
    backward = rising * sums_along(falling * over_modes(dgate), lower)
    forward_parts = split(forward)
    weight_diag = lane_chan * weight_lane
    conv = dot_split(weight_diag, forward_parts)
    dmixed = dot_split(weight_diag, split(backward))
    steps = iota((chans, span), 1).astype(F32)
    apart = split((forward - mixed_rows) * backward)
    ones = jnp.ones((HALF, span), jnp.bfloat16)
    apart_lane = (dot(ones, apart[0], nt, None) + dot(ones, apart[1], nt, None))[0:1]
    half_buf[here, 2 * blocks : 6 * blocks] = jnp.concatenate(
        [
            diagonal_rows(dot_split(mixed * (float(span) - steps), rising_parts, nt)) * chunk_decay,
            diagonal_rows(dot_split(dgate * steps, falling_parts, nt)),
            diagonal_rows(dot_split(dgate, forward_parts, nt)),
            fold(apart_lane),
        ],
        axis=0,
    )
    near_copies = same_place(half_buf.at[here, rest], "near", plane_peer, near_ways)
    start(near_copies)

    @pl.when(zh == 1)
    def _():
        pl.semaphore_wait(sems["first"], count_line((CLOSE, -CLOSE)))
        greet_line(sems["second"], (CLOSE + 1, -CLOSE - 1))

    rate8 = jnp.concatenate([rate4, rate4], axis=0)
    is_state = iota((2 * blocks, LANES), 0) < blocks

    def decay(length, if_state, if_other):
        away = jnp.where(is_state, if_state, if_other).astype(F32)
        power = jnp.exp(-float(length) * rate8 * jnp.maximum(away, 0.0))
        return jnp.where(away >= 0.0, power, 0.0)

    group_len = span * nb
    to_own, to_opp = [], []
    for px in range(nx):
        ahead = nzh * (x - px)
        to_own.append(decay(group_len, ahead - 1, -ahead - 1))
        to_opp.append(decay(group_len, ahead - 2 * zh, -ahead + 2 * zh - 2))
    inside = decay(span, near, nb - 1 - near)
    use = jnp.concatenate([weight4, weight4 * chunk_decay], axis=0)

    def group_states(px):
        run = jnp.zeros_like(rate4)
        back = run
        before = run
        after = run
        for i in range(nb):
            before = jnp.where(near == i, run, before)
            run = chunk_decay * run + half_buf[px * nb + i, 0:blocks]
            j = nb - 1 - i
            after = jnp.where(near == j, back, after)
            back = chunk_decay * back + half_buf[px * nb + j, blocks : 2 * blocks]
        return jnp.concatenate([before, after], axis=0), jnp.concatenate([run, back], axis=0)

    arrive(plane_copies)
    far_states = jnp.zeros_like(rate8)
    twin_states = jnp.zeros_like(rate8)
    from_near = jnp.zeros_like(rate8)
    for px in range(nx):
        around, states = group_states(px)
        from_near = jnp.where(x == px, around, from_near)
        far_states = far_states + to_own[px] * states
        twin_states = twin_states + to_opp[px] * states
    state_buf[zh] = twin_states
    twin_copies = [make(state_buf.at[zh], state_buf.at[zh], "twin", 0, twin)]

    @pl.when(zh == 1)
    def _():
        start(twin_copies)
        pl.semaphore_wait(sems["second"], count_line((CLOSE + 1, -CLOSE - 1)))
        start_line()

    def chained(pieces, length):
        total = pieces[0]
        for i in range(1, len(pieces)):
            total = chain(total, pieces[i], i, length, rate4)
        return total

    def piece(rows):
        return tuple(rows[j * blocks : (j + 1) * blocks] for j in range(6))

    arrive(near_copies)
    pieces = [piece(half_buf[x * nb + i]) for i in range(nb)]
    tuple_buf[far] = jnp.concatenate(chained(pieces, span), axis=0)
    target = {"ctx": jnp.where(same_half, member(near)["ctx"], twin["ctx"]), "ch": zlo}
    tuple_copy = make(tuple_buf.at[far], tuple_buf.at[far], "tuple", far, target)
    pass_copy = make(tuple_buf.at[opp_far], tuple_buf.at[opp_far], "tuple", opp_far, member(near))
    hands_on = jnp.logical_not(collects)
    passes = jnp.logical_and(same_half, hands_on)
    crosses = jnp.logical_not(same_half)
    pl.when(jnp.logical_or(passes, jnp.logical_and(crosses, zh == 1)))(tuple_copy.start)

    two = per_core // 2
    begin = core * per_core

    def across(slots, rows, cols):
        return w_buf.at[pl.ds(slots, two), :, rows, cols]

    x_peers = [(way, 0, 0) for way in x_ways]
    y_peers = [(0, way, 0) for way in y_ways]
    my_part = (part_rows(half), columns(column, 1))
    w2_copies = same_place(across(begin, *my_part), "w2", plane_peer, x_peers)
    w2_copies += same_place(across(begin + two, *my_part), "w2", plane_peer, y_peers, nx - 1)
    w3_copies = []
    for i in range(nx // 2):
        view = across(begin, pl.ds(0, 2 * HALF), columns(i * ny + y, 1))
        w3_copies += same_place(view, "w3", plane_peer, y_peers, i * (ny - 1))
    view = across(begin + two, part_rows(half), columns(lax.rem(x, nx // 2) * ny, ny))
    w3_copies += same_place(view, "w3", plane_peer, x_peers, nx // 2 * (ny - 1))
    whole = w_buf.at[pl.ds(begin, per_core)]
    w4_copies = [make(whole, whole, "w4", 0, sibling)]

    pl.when(core == 0)(own_part.wait)
    pl.when(core != 0)(wz_copies[0].wait_recv)
    arrive(wz_copies[1:])
    start(w2_copies)
    start(kv_copies)
    arrive(w2_copies)
    start(w3_copies)
    arrive(twin_copies)

    @pl.when(zh == 0)
    def _():
        start(twin_copies)

    states = use * (from_near + inside * (far_states + state_buf[1 - zh]))
    conv = conv + dot_split(lane_chan * unfold(states[:blocks]), falling_parts)
    dmixed = dmixed + dot_split(lane_chan * unfold(states[blocks:]), rising_parts)
    late_buf[0, 0] = (up_f * conv).astype(jnp.bfloat16)
    late_buf[0, 1] = dmixed.astype(jnp.bfloat16)
    late_copies = [make(late_buf.at[0], late_buf.at[k], "late", k - 1, line_peer(k)) for k in line_ways]
    start(late_copies)
    dz_buf[0, 0] = late_buf[0, 0]
    dz_buf[0, 1] = (dmixed * value_f).astype(jnp.bfloat16)
    dz_buf[0, 2] = (dmixed * key_f).astype(jnp.bfloat16)

    pl.when(jnp.logical_and(crosses, zh == 0))(tuple_copy.start)

    @pl.when(passes)
    def _():
        pass_copy.wait_recv()
        pass_copy.start()

    arrive(w3_copies)
    start(w4_copies)

    def hand_out(way, index):
        return pltpu.make_async_remote_copy(
            src_ref=total_buf,
            dst_ref=total_buf,
            send_sem=sems["total_send"].at[index],
            recv_sem=sems["total_recv"].at[0],
            device_id=plane_peer(way),
            device_id_type=MESH,
        )

    total_copies = [hand_out(way, i) for i, way in enumerate(near_ways)]

    @pl.when(collects)
    def _():
        for a in range(na):
            arrived = make(tuple_buf.at[a], tuple_buf.at[a], "tuple", a, twin)
            pl.when(far != a)(arrived.wait_recv)
        whole_run = chained([piece(tuple_buf[a]) for a in range(na)], group_len)
        total_buf[...] = jnp.concatenate(whole_run[4:], axis=0)
        start(total_copies)

    arrive(kv_copies)
    arrive(w4_copies)
    arrive(late_copies)
    for k in line_ways:
        dmixed_k = late_buf[k, 1].astype(F32)
        dz_buf[k, 0] = late_buf[k, 0]
        dz_buf[k, 1] = (dmixed_k * raw_buf[k, 2].astype(F32)).astype(jnp.bfloat16)
        dz_buf[k, 2] = (dmixed_k * raw_buf[k, 1].astype(F32)).astype(jnp.bfloat16)
    rows = nzl * 3 * chans
    product = dot(
        dz_buf[...].reshape(rows, span), w_buf[...].reshape(rows, d_len), ((0,), (0,)), None
    )
    out_ref[...] = product.astype(jnp.bfloat16).T

    pl.when(hands_on)(total_copies[0].wait_recv)
    total = total_buf[...]
    sums = dot_nt(
        lane_mode,
        jnp.concatenate([lane_chan * unfold(total[:blocks]), lane_chan * unfold(total[blocks:])], axis=0),
    )
    same, apart = sums[:, :chans], sums[:, chans:]
    scale = 1.0 / math.sqrt(float(token_count))
    gres_ref[...] = same * gain * scale
    glog_ref[...] = weight * (0.5 * same - rates * apart) * scale

    pl.when(core != 0)(wz_copies[0].wait_send)
    pl.when(hands_on)(tuple_copy.wait_send)
    pl.when(passes)(pass_copy.wait_send)

    @pl.when(collects)
    def _():
        for copy in total_copies:
            copy.wait_send()

    for copies in (
        plane_copies,
        near_copies,
        twin_copies,
        wz_copies[1:],
        kv_copies,
        late_copies,
        w2_copies,
        w3_copies,
        w4_copies,
    ):
        for copy in copies:
            copy.wait_send()


def finish(out_in, gres_in, glog_in, out_ref, gres_ref, glog_ref):
    out_ref[...] = out_in[...]
    gres_ref[...] = gres_in[...]
    glog_ref[...] = glog_in[...]


def per_device(dims, queries, keys, values, upstream, residues, rates, w_in):
    nx, nzh, ny, nco, nzl = dims
    nb, na = ny * nco, nx * nzh
    chans, span = queries.shape
    modes = residues.shape[1]
    d_len = w_in.shape[2] // nzl
    pairs = chans * modes
    blocks = pairs // LANES
    vmem = pl.BlockSpec(memory_space=pltpu.VMEM)
    counts = {
        "plane": nx * nb - 1,
        "near": nb - 1,
        "tuple": na,
        "total": nb - 1,
        "twin": 1,
        "wz": nzl // nco,
        "kv": nzl - 1,
        "late": nzl - 1,
        "w2": nx + ny - 2,
        "w3": nx // 2 * (ny - 1) + nx - 1,
        "w4": 1,
    }
    semaphores = {"load": 6, "own": 1}
    for name, count in counts.items():
        semaphores[name + "_send"] = count
        semaphores[name + "_recv"] = count
    arrays = [
        pltpu.with_memory_space_constraint(array, pltpu.HBM)
        for array in (queries, keys, values, upstream, residues.T, rates.T, w_in)
    ]
    results = pl.pallas_call(
        functools.partial(kernel, dims, span * na * nb, (*semaphores, "first", "second")),
        out_shape=(
            jax.ShapeDtypeStruct((d_len, span), jnp.bfloat16),
            jax.ShapeDtypeStruct((modes, chans), F32),
            jax.ShapeDtypeStruct((modes, chans), F32),
        ),
        in_specs=[pl.BlockSpec(memory_space=pltpu.HBM)] * 7,
        out_specs=(vmem, vmem, vmem),
        scratch_shapes=[
            pltpu.VMEM((2, modes, chans), F32),
            pltpu.VMEM((nzl, 4, chans, span), jnp.bfloat16),
            pltpu.VMEM((nx * nb, 6 * blocks, LANES), F32),
            pltpu.VMEM((nzh, 2 * blocks, LANES), F32),
            pltpu.VMEM((na, 6 * blocks, LANES), F32),
            pltpu.VMEM((2 * blocks, LANES), F32),
            pltpu.VMEM((nzl, 2, chans, span), jnp.bfloat16),
            pltpu.VMEM((nzl, 3, chans, span), jnp.bfloat16),
            pltpu.VMEM((nzl, 3, chans, d_len), jnp.bfloat16),
        ]
        + [pltpu.SemaphoreType.DMA((count,)) for count in semaphores.values()]
        + [pltpu.SemaphoreType.REGULAR] * 2,
        compiler_params=pltpu.CompilerParams(
            collective_id=0, has_side_effects=True, vmem_limit_bytes=40 * 1024 * 1024
        ),
        cost_estimate=pl.CostEstimate(
            flops=2 * 3 * chans * nzl * d_len * span, bytes_accessed=2 * w_in.size, transcendentals=0
        ),
    )(*arrays)
    grad_input, grad_residues, grad_lograte = pl.pallas_call(
        finish,
        out_shape=(
            jax.ShapeDtypeStruct((d_len, span), jnp.bfloat16),
            jax.ShapeDtypeStruct((modes, chans), F32),
            jax.ShapeDtypeStruct((modes, chans), F32),
        ),
        in_specs=[vmem] * 3,
        out_specs=(vmem,) * 3,
        compiler_params=pltpu.CompilerParams(vmem_limit_bytes=4 * 1024 * 1024),
    )(*results)
    return grad_input, grad_residues.T, grad_lograte.T


def solution(mesh, dims=(4, 2, 4, 2, 8)):
    return jax.shard_map(
        functools.partial(per_device, dims),
        mesh=mesh,
        in_specs=(
            P("ch", "ctx"),
            P("ch", "ctx"),
            P("ch", "ctx"),
            P("ch", "ctx"),
            P("ch", None),
            P("ch", None),
            P(None, "ch", None),
        ),
        out_specs=(P("ch", "ctx"), P("ch", None), P("ch", None)),
        check_vma=False,
    )
```
